32 devices in a mesh: tile: 8 (over z, x), chan: 4 (over y, core).
Axes of the slice: x: 2, y: 2, z: 4, core: 2. Of those that a mesh axis runs over, the one named last changes fastest.
Arguments:
- tiles: bfloat16 [8, 128, 16, 16, 128], P('tile'), may hold values from -6 to 6
- orientation: int32 [8], P('tile'), may hold values from 0 to 3
- weight: bfloat16 [3, 3, 128, 128], P(None, None, None, 'chan'), may hold values from -0.1875 to 0.1875
- grad_out: bfloat16 [8, 128, 16, 16, 128], P('tile'), may hold values from -6 to 6
Outputs:
- conv_out: bfloat16 [8, 128, 16, 16, 128], P('tile', None, None, None, 'chan')
- grad_input: bfloat16 [8, 128, 16, 16, 128], P('tile', None, None, None, 'chan')
- grad_weight: float32 [3, 3, 128, 128], P(None, None, None, 'chan')
The draws below stay inside these ranges and needn't reach their ends.
All inputs are finite; a program needn't handle non-finite values.
Results may differ from the reference program's by a relative error of at most 0.0034.
Values may be sent and summed in bfloat16 or wider, within the bound.
No kernel may reach another device: no remote copies, remote signals or barrier semaphores. Data moves between devices by JAX's collectives and lax.ppermute only.
A program may use at most 128 MiB of HBM per device.

```python
import math
from functools import partial
import jax
import jax.numpy as jnp
from jax import lax

CHANNELS = 128
SIDE = 16
BATCH = 128
N_TILE = 8


def place_ends(values, key, low, high):
    index_at = [jax.random.randint(jax.random.fold_in(key, axis), (), 0, length) for axis, length in enumerate(values.shape)]
    widest = values.shape.index(max(values.shape))
    beside = index_at[:widest] + [(index_at[widest] + 1) % values.shape[widest]] + index_at[widest + 1:]
    return values.at[tuple(index_at)].set(low).at[tuple(beside)].set(high)


def level_of(key, extent, shards, least, largest):
    factor_of = 1.0
    for dim, parts in shards:
        heights = jax.random.uniform(jax.random.fold_in(jax.random.fold_in(key, 6), dim), (parts,), jnp.float32, least / len(shards), largest / len(shards))
        factor_of = factor_of * jnp.repeat(jnp.exp(heights), extent[dim] // parts).reshape((-1,) + (1,) * (len(extent) - 1 - dim))
    return factor_of


def centred(own_key, extent, scale, reach, split=(), held_as=jnp.bfloat16):
    factor_of = level_of(own_key, extent, split, -0.22, 0.18) if split else 1.0
    values = jax.random.normal(own_key, extent, jnp.float32) * scale * factor_of
    return jnp.minimum(jnp.maximum(values, -reach), reach).astype(held_as)


def setup_inputs(seed: int = 0) -> dict:
    key_list = jax.random.split(jax.random.key(seed), 5)
    tiles = centred(key_list[0], (N_TILE, BATCH, SIDE, SIDE, CHANNELS), 1.0, 6.0, ((0, 8),))
    orientation = place_ends(jax.random.randint(key_list[1], (N_TILE,), 0, 4), jax.random.fold_in(key_list[1], 1), 0, 3).astype(jnp.int32)
    weight = centred(key_list[2], (3, 3, CHANNELS, CHANNELS), (9 * CHANNELS) ** -0.5, 0.1875, ((3, 4),))
    grad_out = centred(key_list[3], (N_TILE, BATCH, SIDE, SIDE, CHANNELS), 1.0, 6.0, ((0, 8),))
    return {"tiles": tiles, "orientation": orientation, "weight": weight, "grad_out": grad_out}


def turn_block(block, quarters):
    branches = [partial(jnp.rot90, k=amount, axes=(1, 2)) for amount in range(4)]
    return lax.switch(quarters, branches, block)

def forward_all(field_f32, weight_f32, orientation):
    along_count = N_TILE // 2
    global_tiles = lax.map(lambda entries: turn_block(entries[0], (4 - entries[1]) % 4), (field_f32, orientation))
    equator_band = global_tiles.reshape(along_count, 2, BATCH, SIDE, SIDE, CHANNELS)
    equator_band = equator_band.transpose(2, 1, 3, 0, 4, 5).reshape(BATCH, 2 * SIDE, along_count * SIDE, CHANNELS)
    equator_band = jnp.concatenate([equator_band[:, :, -1:], equator_band, equator_band[:, :, :1]], axis=2)
    equator_band = jnp.pad(equator_band, ((0, 0), (1, 1), (0, 0), (0, 0)))
    corner_mask = jnp.ones((SIDE + 2, SIDE + 2), jnp.float32)
    corner_mask = corner_mask.at[0, 0].set(0.0).at[0, -1].set(0.0).at[-1, 0].set(0.0).at[-1, -1].set(0.0)

    def tile_conv(entries):
        tile_id, quarters = entries
        across = (tile_id % 2).astype(jnp.int32)
        beside_all = (tile_id // 2).astype(jnp.int32)
        start = (jnp.zeros((), jnp.int32), across * SIDE, beside_all * SIDE, jnp.zeros((), jnp.int32))
        padded_block = lax.dynamic_slice(equator_band, start, (BATCH, SIDE + 2, SIDE + 2, CHANNELS))
        padded_block = padded_block * corner_mask[None, :, :, None]
        local_block = turn_block(padded_block, quarters)
        return lax.conv_general_dilated(local_block, weight_f32, (1, 1), 'VALID', dimension_numbers=('NHWC', 'HWIO', 'NHWC'), precision=lax.Precision.HIGHEST)
    return lax.map(tile_conv, (jnp.arange(N_TILE, dtype=jnp.int32), orientation))

def reference(tiles, orientation, weight, grad_out):
    field_f32 = tiles.astype(jnp.float32)
    weight_f32 = weight.astype(jnp.float32)

    def apply_layer(inputs_f32, weights_f32):
        return forward_all(inputs_f32, weights_f32, orientation)
    output_f32, backward_fn = jax.vjp(apply_layer, field_f32, weight_f32)
    grad_field, grad_filters = backward_fn(grad_out.astype(jnp.float32))
    normalizer = 1.0 / math.sqrt(N_TILE * BATCH * SIDE * SIDE)
    return (output_f32.astype(jnp.bfloat16), grad_field.astype(jnp.bfloat16), grad_filters * normalizer)
```

```python
import math

import jax
import jax.numpy as jnp
from jax import lax
from jax.experimental import pallas as pl
from jax.experimental.pallas import tpu as pltpu
from jax.sharding import PartitionSpec as P

ROWS = 4
COLS = 2
BIG = 56 << 20


def passed_along(value, axis, pairs):
    return lax.ppermute(value, axis, pairs)


def dot_nt(left, right):
    return lax.dot_general(
        left, right, (((1,), (1,)), ((), ())), preferred_element_type=jnp.float32
    )


def dot_nn(left, right):
    return lax.dot_general(
        left, right, (((1,), (0,)), ((), ())), preferred_element_type=jnp.float32
    )


def relay_kernel(field, upstream, pick, field_out, upstream_out, turned_out):
    rows, side, batch, channels = field_out.shape
    for row in range(rows):
        field_out[row] = jnp.swapaxes(field[:, row], 0, 1)
        block = jnp.swapaxes(upstream[:, row], 0, 1)
        upstream_out[row] = block
        turned_out[row] = dot_nt(
            pick[...], block.reshape(side * batch, channels)
        ).astype(jnp.bfloat16)


def relay(field, upstream, pick):
    batch, side, _, channels = field.shape
    share = pick.shape[0]
    rows = 2
    laid = jax.ShapeDtypeStruct((side, side, batch, channels), jnp.bfloat16)
    in_spec = pl.BlockSpec((batch, rows, side, channels), lambda i: (0, i, 0, 0))
    out_spec = pl.BlockSpec((rows, side, batch, channels), lambda i: (i, 0, 0, 0))
    return pl.pallas_call(
        relay_kernel,
        grid=(side // rows,),
        in_specs=[in_spec, in_spec, pl.BlockSpec(memory_space=pltpu.VMEM)],
        out_specs=[
            out_spec,
            out_spec,
            pl.BlockSpec((rows, share, side * batch), lambda i: (i, 0, 0)),
        ],
        out_shape=[
            laid,
            laid,
            jax.ShapeDtypeStruct((side, share, side * batch), jnp.bfloat16),
        ],
        compiler_params=pltpu.CompilerParams(vmem_limit_bytes=BIG),
        cost_estimate=pl.CostEstimate(
            flops=2 * field.size * share, bytes_accessed=8 * field.size, transcendentals=0
        ),
        name="relay",
    )(field, upstream, pick)


def fetch_edges(place, source, held, sems):
    side = held.shape[1]
    for edge in range(3):
        for pos in range(side):
            pixel = place[edge, 0] + pos * place[edge, 1]
            pltpu.make_async_copy(
                source.at[pixel], held.at[edge, pos], sems.at[edge]
            ).start()


def wait_edge(source, held, sems, edge):
    side = held.shape[1]
    pltpu.make_async_copy(
        source.at[pl.ds(0, side)], held.at[edge], sems.at[edge]
    ).wait()


def later(value, width):
    empty = jnp.zeros((value.shape[0], width), value.dtype)
    return jnp.concatenate([empty, value[:, :-width]], axis=1)


def earlier(value, width):
    empty = jnp.zeros((value.shape[0], width), value.dtype)
    return jnp.concatenate([value[:, width:], empty], axis=1)


def edge_kernel(
    place, conv_tap, grad_tap, field, upstream, weight, whole, pick,
    east, west, across, field_edge, upstream_edge, rowed, field_sem, upstream_sem,
):
    share, channels = pick.shape
    taps = weight.shape[0]
    side, batch = field_edge.shape[1:3]
    fetch_edges(place, field, field_edge, field_sem)
    fetch_edges(place, upstream, upstream_edge, upstream_sem)
    for tap in range(taps):
        rowed[tap] = dot_nt(pick[...], whole[tap]).astype(jnp.bfloat16)

    def gathered(product):
        return (
            later(product[:share], batch)
            + product[share : 2 * share]
            + earlier(product[2 * share : 3 * share], batch)
        )

    for edge, out in enumerate((east, west, across)):
        wait_edge(field, field_edge, field_sem, edge)
        wait_edge(upstream, upstream_edge, upstream_sem, edge)
        filters = jnp.concatenate([weight[conv_tap[edge, d]] for d in range(3)], axis=0)
        product = dot_nt(filters, field_edge[edge].reshape(side * batch, channels))
        out[0:share] = gathered(product).astype(jnp.bfloat16)
        filters = jnp.concatenate(
            [rowed[grad_tap[edge, 2 - d]] for d in range(3)] + [pick[...]], axis=0
        )
        product = dot_nt(filters, upstream_edge[edge].reshape(side * batch, channels))
        out[share : 2 * share] = gathered(product).astype(jnp.bfloat16)
        out[2 * share :] = product[3 * share :].astype(jnp.bfloat16)


def edge_messages(place, conv_tap, grad_tap, field, upstream, weight, whole, pick, side):
    pixels, batch, channels = field.shape
    share = pick.shape[0]
    message = jax.ShapeDtypeStruct((3 * share, side * batch), jnp.bfloat16)
    smem = pl.BlockSpec(memory_space=pltpu.SMEM)
    vmem = pl.BlockSpec(memory_space=pltpu.VMEM)
    anywhere = pl.BlockSpec(memory_space=pl.ANY)
    return pl.pallas_call(
        edge_kernel,
        in_specs=[smem] * 3 + [anywhere] * 2 + [vmem] * 3,
        out_specs=[vmem] * 3,
        out_shape=[message] * 3,
        scratch_shapes=[
            pltpu.VMEM((3, side, batch, channels), jnp.bfloat16),
            pltpu.VMEM((3, side, batch, channels), jnp.bfloat16),
            pltpu.VMEM((weight.shape[0], share, channels), jnp.bfloat16),
            pltpu.SemaphoreType.DMA((3,)),
            pltpu.SemaphoreType.DMA((3,)),
        ],
        compiler_params=pltpu.CompilerParams(vmem_limit_bytes=BIG),
        cost_estimate=pl.CostEstimate(
            flops=6 * 7 * share * side * batch * channels,
            bytes_accessed=12 * side * batch * channels,
            transcendentals=0,
        ),
        name="edges",
    )(place, conv_tap, grad_tap, field, upstream, weight, whole, pick)


def filters_kernel(turned, field, out, padded, total, sem):
    step = pl.program_id(0)
    rows, side, batch, channels = field.shape
    share = turned.shape[1]
    width = side * batch

    @pl.when(step == 0)
    def _():
        copy = pltpu.make_async_copy(
            turned, padded.at[pl.ds(1, side), :, pl.ds(batch, width)], sem
        )
        copy.start()
        padded[0] = jnp.zeros(padded.shape[1:], padded.dtype)
        padded[side + 1] = jnp.zeros(padded.shape[1:], padded.dtype)
        column = jnp.zeros((side, share, batch), padded.dtype)
        padded[1 : side + 1, :, 0:batch] = column
        padded[1 : side + 1, :, width + batch :] = column
        total[...] = jnp.zeros_like(total)
        copy.wait()

    first = step * rows
    parts = []
    for col in range(3):
        part = padded[pl.ds(first, rows + 2), :, (2 - col) * batch : (2 - col) * batch + width]
        parts.append(part.reshape((rows + 2) * share, width))
    left = jnp.concatenate(parts, axis=0)
    right = jnp.concatenate([field[row].reshape(width, channels) for row in range(rows)], axis=1)
    total[...] += dot_nn(left, right)

    @pl.when(step == pl.num_programs(0) - 1)
    def _():
        for row_tap in range(3):
            for col_tap in range(3):
                value = jnp.zeros((share, channels), jnp.float32)
                for row in range(rows):
                    start = col_tap * (rows + 2) * share + (row + 2 - row_tap) * share
                    value += total[
                        start : start + share, row * channels : (row + 1) * channels
                    ]
                out[row_tap * 3 + col_tap] = value


def filter_terms(turned, field):
    side, _, batch, channels = field.shape
    share = turned.shape[1]
    rows = 2
    return pl.pallas_call(
        filters_kernel,
        grid=(side // rows,),
        in_specs=[
            pl.BlockSpec(memory_space=pl.ANY),
            pl.BlockSpec((rows, side, batch, channels), lambda i: (i, 0, 0, 0)),
        ],
        out_specs=pl.BlockSpec((9, share, channels), lambda i: (0, 0, 0)),
        out_shape=jax.ShapeDtypeStruct((9, share, channels), jnp.float32),
        scratch_shapes=[
            pltpu.VMEM((side + 2, share, (side + 2) * batch), jnp.bfloat16),
            pltpu.VMEM((3 * (rows + 2) * share, rows * channels), jnp.float32),
            pltpu.SemaphoreType.DMA,
        ],
        compiler_params=pltpu.CompilerParams(vmem_limit_bytes=BIG),
        cost_estimate=pl.CostEstimate(
            flops=24 * share * field.size, bytes_accessed=3 * field.size, transcendentals=0
        ),
        name="filters",
    )(turned, field)


def seam_filters_kernel(
    scale, place, conv_tap, field, inner, east, west, across, out, field_edge, sem
):
    share = out.shape[1]
    side, batch, channels = field_edge.shape[1:]
    fetch_edges(place, field, field_edge, sem)
    out[...] = inner[...]
    for edge, message in enumerate((east, west, across)):
        wait_edge(field, field_edge, sem, edge)
        turned = message[2 * share :]
        left = jnp.concatenate([earlier(turned, batch), turned, later(turned, batch)], axis=0)
        terms = dot_nn(left, field_edge[edge].reshape(side * batch, channels))
        for d in range(3):
            out[conv_tap[edge, d]] += terms[d * share : (d + 1) * share]
    out[...] = out[...] * scale


def seam_filters(scale, place, conv_tap, field, inner, messages, side):
    _, batch, channels = field.shape
    smem = pl.BlockSpec(memory_space=pltpu.SMEM)
    vmem = pl.BlockSpec(memory_space=pltpu.VMEM)

    def body(*refs):
        seam_filters_kernel(scale, *refs)

    return pl.pallas_call(
        body,
        in_specs=[smem] * 2 + [pl.BlockSpec(memory_space=pl.ANY)] + [vmem] * 4,
        out_specs=vmem,
        out_shape=jax.ShapeDtypeStruct(inner.shape, jnp.float32),
        scratch_shapes=[
            pltpu.VMEM((3, side, batch, channels), jnp.bfloat16),
            pltpu.SemaphoreType.DMA((3,)),
        ],
        compiler_params=pltpu.CompilerParams(vmem_limit_bytes=BIG),
        cost_estimate=pl.CostEstimate(
            flops=18 * inner.shape[1] * side * batch * channels,
            bytes_accessed=6 * side * batch * channels,
            transcendentals=0,
        ),
        name="seam_filters",
    )(place, conv_tap, field, inner, *messages)


def conv_kernel(mirrored, source, weight, whole, pick, out, padded, spread, sems):
    step = pl.program_id(0)
    _, side, batch, channels = source.shape
    share = pick.shape[0]
    in_rows, in_cols = ROWS + 2, COLS + 2

    def row_copy(row):
        return pltpu.make_async_copy(
            source.at[row], padded.at[row + 1, pl.ds(1, side)], sems.at[row]
        )

    @pl.when(step == 0)
    def _():
        for row in range(side):
            row_copy(row).start()
        edge = jnp.zeros((side + 2, batch, channels), padded.dtype)
        padded[0] = edge
        padded[side + 1] = edge
        tile = jnp.zeros((batch, channels), padded.dtype)

        @pl.loop(1, side + 1)
        def _(row):
            padded[row, 0] = tile
            padded[row, side + 1] = tile

        spread[...] = jnp.zeros_like(spread)
        for tap in range(9):
            if mirrored:
                block = dot_nt(pick[...], whole[8 - tap]).astype(jnp.bfloat16)
            else:
                block = weight[tap]
            for row in range(ROWS):
                for col in range(COLS):
                    at = (row + tap // 3) * in_cols + col + tap % 3
                    to = row * COLS + col
                    spread[
                        to * share : (to + 1) * share, at * channels : (at + 1) * channels
                    ] = block
        row_copy(0).wait()

    for row in range(ROWS):
        ahead = step * ROWS + row + 1

        @pl.when(ahead < side)
        def _():
            row_copy(ahead).wait()

    first = step * ROWS

    @pl.loop(0, side // (2 * COLS))
    def _(pair):
        rights = []
        for half in range(2):
            start = pair * (2 * COLS) + half * COLS
            rights.append(
                jnp.concatenate(
                    [
                        padded[first + row, start + col]
                        for row in range(in_rows)
                        for col in range(in_cols)
                    ],
                    axis=1,
                )
            )
        result = dot_nt(spread[...], jnp.concatenate(rights, axis=0))
        for half in range(2):
            for row in range(ROWS):
                for col in range(COLS):
                    to = row * COLS + col
                    out[row, pair * (2 * COLS) + half * COLS + col] = result[
                        to * share : (to + 1) * share, half * batch : (half + 1) * batch
                    ].astype(jnp.bfloat16)


def convolved(mirrored, source, weight, whole, pick):
    side, _, batch, channels = source.shape
    share = pick.shape[0]
    vmem = pl.BlockSpec(memory_space=pltpu.VMEM)

    def body(*refs):
        conv_kernel(mirrored, *refs)

    return pl.pallas_call(
        body,
        grid=(side // ROWS,),
        in_specs=[pl.BlockSpec(memory_space=pl.ANY)] + [vmem] * 3,
        out_specs=pl.BlockSpec((ROWS, side, share, batch), lambda i: (i, 0, 0, 0)),
        out_shape=jax.ShapeDtypeStruct((side, side, share, batch), jnp.bfloat16),
        scratch_shapes=[
            pltpu.VMEM((side + 2, side + 2, batch, channels), jnp.bfloat16),
            pltpu.VMEM(
                (ROWS * COLS * share, (ROWS + 2) * (COLS + 2) * channels), jnp.bfloat16
            ),
            pltpu.SemaphoreType.DMA((side,)),
        ],
        compiler_params=pltpu.CompilerParams(vmem_limit_bytes=BIG),
        cost_estimate=pl.CostEstimate(
            flops=48 * share * source.size, bytes_accessed=3 * source.size, transcendentals=0
        ),
        name="grad_conv" if mirrored else "conv",
    )(source, weight, whole, pick)


def border_kernel(
    place, conv_in, grad_in, east, west, across, conv_out, grad_out,
    conv_held, grad_held, in_sem, out_sem,
):
    side, _, share, batch = conv_held.shape

    def pieces(source, target, sem):
        inner = pl.ds(1, side - 2)
        return [
            pltpu.make_async_copy(source.at[where], target.at[where], sem.at[index])
            for index, where in enumerate(
                ((0,), (side - 1,), (inner, 0), (inner, side - 1))
            )
        ]

    def both(step):
        if step == 0:
            return pieces(conv_in, conv_held, in_sem.at[0]) + pieces(
                grad_in, grad_held, in_sem.at[1]
            )
        return pieces(conv_held, conv_out, out_sem.at[0]) + pieces(
            grad_held, grad_out, out_sem.at[1]
        )

    for copy in both(0):
        copy.start()
    for copy in both(0):
        copy.wait()
    for edge, message in enumerate((east, west, across)):
        for pos in range(side):
            pixel = place[edge, 0] + pos * place[edge, 1]
            row, col = pixel // side, pixel % side
            for part, held in enumerate((conv_held, grad_held)):
                term = message[
                    part * share : (part + 1) * share, pos * batch : (pos + 1) * batch
                ]
                held[row, col] = (
                    held[row, col].astype(jnp.float32) + term.astype(jnp.float32)
                ).astype(jnp.bfloat16)
    for copy in both(1):
        copy.start()
    for copy in both(1):
        copy.wait()


def with_borders(place, conv, grad, messages):
    smem = pl.BlockSpec(memory_space=pltpu.SMEM)
    vmem = pl.BlockSpec(memory_space=pltpu.VMEM)
    anywhere = pl.BlockSpec(memory_space=pl.ANY)
    whole = jax.ShapeDtypeStruct(conv.shape, conv.dtype)
    return pl.pallas_call(
        border_kernel,
        in_specs=[smem] + [anywhere] * 2 + [vmem] * 3,
        out_specs=[anywhere] * 2,
        out_shape=[whole] * 2,
        scratch_shapes=[
            pltpu.VMEM(conv.shape, conv.dtype),
            pltpu.VMEM(conv.shape, conv.dtype),
            pltpu.SemaphoreType.DMA((2, 4)),
            pltpu.SemaphoreType.DMA((2, 4)),
        ],
        input_output_aliases={1: 0, 2: 1},
        compiler_params=pltpu.CompilerParams(vmem_limit_bytes=BIG),
        name="borders",
    )(place, conv, grad, *messages)


def stored(turn, row, col, last):
    rows = jnp.stack([row, last - col, last - row, col])
    cols = jnp.stack([col, row, last - col, last - row])
    return jnp.take(rows, turn), jnp.take(cols, turn)


def edge_tables(turns, position, side):
    last = side - 1
    lower = position % 2
    zero = jnp.zeros((), jnp.int32)
    full = jnp.full((), last, jnp.int32)
    edge_row = last * (1 - lower)

    def pixel(row, col):
        r, c = stored(turns[0], row, col, last)
        return r * side + c

    place = []
    for start, end in (
        ((zero, full), (zero + 1, full)),
        ((zero, zero), (zero + 1, zero)),
        ((edge_row, zero), (edge_row, zero + 1)),
    ):
        place.append(jnp.stack([pixel(*start), pixel(*end) - pixel(*start)]))

    def taps(turn, cells):
        out = []
        for row, col in cells:
            r, c = stored(turn, row, col, 2)
            out.append(r * 3 + c)
        return jnp.stack(out)

    ones = [zero + d for d in range(3)]
    two = zero + 2
    conv_tap = jnp.stack(
        [
            taps(turns[1], [(d, zero) for d in ones]),
            taps(turns[2], [(d, two) for d in ones]),
            taps(turns[3], [(2 * lower, d) for d in ones]),
        ]
    )
    grad_tap = jnp.stack(
        [
            taps(turns[0], [(d, two) for d in ones]),
            taps(turns[0], [(d, zero) for d in ones]),
            taps(turns[0], [(2 - 2 * lower, d) for d in ones]),
        ]
    )
    return jnp.stack(place), conv_tap, grad_tap


def per_device(tiles, orientation, weight, grad_out):
    field = tiles[0]
    upstream = grad_out[0]
    batch, side, _, channels = field.shape
    share = weight.shape[3]
    position = lax.axis_index("tile").astype(jnp.int32)
    chan_index = lax.axis_index("chan").astype(jnp.int32)
    count = lax.axis_size("tile")
    eastward = [(i, (i + 2) % count) for i in range(count)]
    westward = [(i, (i - 2) % count) for i in range(count)]
    acrossward = [(i, i ^ 1) for i in range(count)]

    code = orientation.astype(jnp.bfloat16)
    codes = [
        lax.ppermute(code, "tile", pairs) for pairs in (westward, eastward, acrossward)
    ]
    turns = [orientation[0]] + [c[0].astype(jnp.int32) for c in codes]
    place, conv_tap, grad_tap = edge_tables(turns, position, side)

    own = weight.transpose(0, 1, 3, 2).reshape(9, share, channels)
    whole = lax.all_gather(own, "chan", axis=1, tiled=True)
    pick = (
        lax.broadcasted_iota(jnp.int32, (share, channels), 0) + chan_index * share
        == lax.broadcasted_iota(jnp.int32, (share, channels), 1)
    ).astype(jnp.bfloat16)

    field_laid, upstream_laid, turned = relay(field, upstream, pick)
    field_flat = field_laid.reshape(side * side, batch, channels)
    upstream_flat = upstream_laid.reshape(side * side, batch, channels)
    sends = edge_messages(
        place, conv_tap, grad_tap, field_flat, upstream_flat, own, whole, pick, side
    )
    from_west = lax.ppermute(sends[0], "tile", eastward)
    from_east = lax.ppermute(sends[1], "tile", westward)
    from_across = lax.ppermute(sends[2], "tile", acrossward)
    messages = (from_east, from_west, from_across)

    inner = filter_terms(turned, field_laid)
    grad = convolved(True, upstream_laid, own, whole, pick)
    scale = 1.0 / math.sqrt(count * batch * side * side)
    total = seam_filters(scale, place, conv_tap, field_flat, inner, messages, side)
    conv = convolved(False, field_laid, own, whole, pick)
    bit = 1
    while bit < count:
        pairs = [(i, i ^ bit) for i in range(count)]
        total = total + lax.ppermute(total, "tile", pairs)
        bit *= 2
    conv, grad = with_borders(place, conv, grad, messages)
    conv_out = conv.transpose(3, 0, 1, 2)[None]
    grad_input = grad.transpose(3, 0, 1, 2)[None]
    grad_weight = total.reshape(3, 3, share, channels).transpose(0, 1, 3, 2)
    return conv_out, grad_input, grad_weight


def solution(mesh):
    in_specs = (
        P("tile", None, None, None, None),
        P("tile"),
        P(None, None, None, "chan"),
        P("tile", None, None, None, None),
    )
    out_specs = (
        P("tile", None, None, None, "chan"),
        P("tile", None, None, None, "chan"),
        P(None, None, None, "chan"),
    )
    return jax.shard_map(
        per_device, mesh=mesh, in_specs=in_specs, out_specs=out_specs, check_vma=False
    )
```

```python
import math

import jax
import jax.numpy as jnp
from jax import lax
from jax.experimental import pallas as pl
from jax.experimental.pallas import tpu as pltpu
from jax.sharding import PartitionSpec as P

BIG = 56 << 20
FLAT = (((1,), (0,)), ((), ()))
TURNED = (((1,), (1,)), ((), ()))


def dot(left, right, dims):
    return lax.dot_general(left, right, dims, preferred_element_type=jnp.float32)


def stored(turn, row, col, last):

    def chosen(values):
        return jnp.where(
            turn < 2,
            jnp.where(turn == 0, values[0], values[1]),
            jnp.where(turn == 2, values[2], values[3]),
        )

    return (
        chosen((row, last - col, last - row, col)),
        chosen((col, row, last - col, last - row)),
    )


def edge_place(turn, lower, edge, side):
    last = side - 1
    if edge == 0:
        start, after = (0, last), (1, last)
    elif edge == 1:
        start, after = (0, 0), (1, 0)
    else:
        row = last * (1 - lower)
        start, after = (row, 0), (row, 1)
    first = stored(turn, *start, last)
    second = stored(turn, *after, last)
    return first, (second[0] - first[0], second[1] - first[1])


def edge_tap(turn, lower, edge, along, outward):
    if edge == 0:
        cell = (along, 2 if outward else 0)
    elif edge == 1:
        cell = (along, 0 if outward else 2)
    else:
        cell = (2 - 2 * lower if outward else 2 * lower, along)
    row, col = stored(turn, *cell, 2)
    return row * 3 + col


def one_hot(share, channels):
    chan = lax.axis_index("chan").astype(jnp.int32)
    rows = lax.broadcasted_iota(jnp.int32, (share, channels), 0) + chan * share
    cols = lax.broadcasted_iota(jnp.int32, (share, channels), 1)
    return jnp.where(rows == cols, 1.0, 0.0).astype(jnp.bfloat16)


def relay_kernel(field, upstream, field_out, upstream_out, turned_out, shuffle):
    rows, side, batch, channels = field_out.shape
    share = turned_out.shape[1]
    group = 256 // side

    @pl.when(pl.program_id(0) == 0)
    def _():
        to = lax.broadcasted_iota(jnp.int32, (256, 256), 0)
        come = lax.broadcasted_iota(jnp.int32, (256, 256), 1)
        same = (to // group == come % side) & (to % group == come // side)
        shuffle[...] = jnp.where(same, 1.0, 0.0).astype(jnp.bfloat16)

    for source, out in ((upstream, upstream_out), (field, field_out)):
        for start in range(0, batch, group):
            block = jnp.concatenate(
                [
                    source[start : start + group, row].reshape(256, channels)
                    for row in range(rows)
                ],
                axis=1,
            )
            moved = dot(shuffle[...], block, FLAT).astype(jnp.bfloat16)
            for row in range(rows):
                out[row, :, start : start + group] = moved[
                    :, row * channels : (row + 1) * channels
                ].reshape(side, group, channels)
    pick = one_hot(share, channels)
    for row in range(rows):
        turned_out[row] = dot(
            pick, upstream_out[row].reshape(side * batch, channels), TURNED
        ).astype(jnp.bfloat16)


def relay(field, upstream, share):
    batch, side, _, channels = field.shape
    rows = 2
    laid = jax.ShapeDtypeStruct((side, side, batch, channels), jnp.bfloat16)
    in_spec = pl.BlockSpec((batch, rows, side, channels), lambda i: (0, i, 0, 0))
    out_spec = pl.BlockSpec((rows, side, batch, channels), lambda i: (i, 0, 0, 0))
    return pl.pallas_call(
        relay_kernel,
        grid=(side // rows,),
        in_specs=[in_spec, in_spec],
        out_specs=[
            out_spec,
            out_spec,
            pl.BlockSpec((rows, share, side * batch), lambda i: (i, 0, 0)),
        ],
        out_shape=[
            laid,
            laid,
            jax.ShapeDtypeStruct((side, share, side * batch), jnp.bfloat16),
        ],
        scratch_shapes=[pltpu.VMEM((256, 256), jnp.bfloat16)],
        compiler_params=pltpu.CompilerParams(vmem_limit_bytes=BIG),
        cost_estimate=pl.CostEstimate(
            flops=1024 * field.size, bytes_accessed=8 * field.size, transcendentals=0
        ),
        name="relay",
    )(field, upstream)


def fetch_edges(turn, lower, source, held, sems):
    side = held.shape[1]
    for edge in range(3):
        (row, col), (down, right) = edge_place(turn, lower, edge, side)
        for pos in range(side):
            pltpu.make_async_copy(
                source.at[row + pos * down, col + pos * right],
                held.at[edge, pos],
                sems.at[edge],
            ).start()


def wait_edge(source, held, sems, edge):
    pltpu.make_async_copy(source.at[0], held.at[edge], sems.at[edge]).wait()


def later(value, width):
    empty = jnp.zeros((value.shape[0], width), value.dtype)
    return jnp.concatenate([empty, value[:, :-width]], axis=1)


def earlier(value, width):
    empty = jnp.zeros((value.shape[0], width), value.dtype)
    return jnp.concatenate([value[:, width:], empty], axis=1)


def gather_filters(parts, whole):
    taps, share, _ = parts[0].shape
    chan = lax.axis_index("chan").astype(jnp.int32)
    for flip, part in enumerate(parts):
        start = pl.multiple_of((chan ^ flip) * share, share)
        for tap in range(taps):
            whole[tap, pl.ds(start, share)] = part[tap]


def edge_kernel(
    own_turn, east_turn, west_turn, across_turn, field, upstream, weight, *refs
):
    others = refs[:-10]
    east, west, across = refs[-10:-7]
    field_edge, upstream_edge, whole, rowed, field_sem, upstream_sem, _ = refs[-7:]
    taps, share, channels = weight.shape
    side, batch = field_edge.shape[1:3]
    lower = lax.axis_index("tile").astype(jnp.int32) % 2
    turn = own_turn[0]
    fetch_edges(turn, lower, field, field_edge, field_sem)
    fetch_edges(turn, lower, upstream, upstream_edge, upstream_sem)
    pick = one_hot(share, channels)
    gather_filters((weight,) + others, whole)
    for tap in range(taps):
        rowed[tap] = dot(pick, whole[tap], TURNED).astype(jnp.bfloat16)

    def gathered(product):
        return (
            later(product[:share], batch)
            + product[share : 2 * share]
            + earlier(product[2 * share : 3 * share], batch)
        )

    turns = (east_turn[0], west_turn[0], across_turn[0])
    for edge, out in enumerate((east, west, across)):
        wait_edge(field, field_edge, field_sem, edge)
        wait_edge(upstream, upstream_edge, upstream_sem, edge)
        filters = jnp.concatenate(
            [weight[edge_tap(turns[edge], lower, edge, d, False)] for d in range(3)], axis=0
        )
        product = dot(filters, field_edge[edge].reshape(side * batch, channels), TURNED)
        out[0:share] = gathered(product).astype(jnp.bfloat16)
        filters = jnp.concatenate(
            [rowed[edge_tap(turn, lower, edge, 2 - d, True)] for d in range(3)] + [pick],
            axis=0,
        )
        product = dot(filters, upstream_edge[edge].reshape(side * batch, channels), TURNED)
        out[share : 2 * share] = gathered(product).astype(jnp.bfloat16)
        out[2 * share :] = product[3 * share :].astype(jnp.bfloat16)


def edge_messages(turns, field, upstream, weights):
    side, _, batch, channels = field.shape
    taps, share, _ = weights[0].shape
    message = jax.ShapeDtypeStruct((3 * share, side * batch), jnp.bfloat16)
    smem = pl.BlockSpec(memory_space=pltpu.SMEM)
    vmem = pl.BlockSpec(memory_space=pltpu.VMEM)
    anywhere = pl.BlockSpec(memory_space=pl.ANY)
    return pl.pallas_call(
        edge_kernel,
        in_specs=[smem] * 4 + [anywhere] * 2 + [vmem] * len(weights),
        out_specs=[vmem] * 3,
        out_shape=[message] * 3,
        scratch_shapes=[
            pltpu.VMEM((3, side, batch, channels), jnp.bfloat16),
            pltpu.VMEM((3, side, batch, channels), jnp.bfloat16),
            pltpu.VMEM((taps, channels, channels), jnp.bfloat16),
            pltpu.VMEM((taps, share, channels), jnp.bfloat16),
            pltpu.SemaphoreType.DMA((3,)),
            pltpu.SemaphoreType.DMA((3,)),
            pltpu.SMEM((1,), jnp.int32),
        ],
        compiler_params=pltpu.CompilerParams(vmem_limit_bytes=BIG),
        cost_estimate=pl.CostEstimate(
            flops=6 * 7 * share * side * batch * channels,
            bytes_accessed=12 * side * batch * channels,
            transcendentals=0,
        ),
        name="edges",
    )(*turns, field, upstream, *weights)


def filters_kernel(turned, field, out, padded, total, sem):
    step = pl.program_id(0)
    rows, side, batch, channels = field.shape
    share = turned.shape[1]
    width = side * batch

    @pl.when(step == 0)
    def _():
        copy = pltpu.make_async_copy(
            turned, padded.at[pl.ds(1, side), :, pl.ds(batch, width)], sem
        )
        copy.start()
        padded[0] = jnp.zeros(padded.shape[1:], padded.dtype)
        padded[side + 1] = jnp.zeros(padded.shape[1:], padded.dtype)
        column = jnp.zeros((side, share, batch), padded.dtype)
        padded[1 : side + 1, :, 0:batch] = column
        padded[1 : side + 1, :, width + batch :] = column
        total[...] = jnp.zeros_like(total)
        copy.wait()

    first = step * rows
    cols = 4
    for start in range(0, side, cols):
        parts = []
        for tap in range(3):
            at = (start + 2 - tap) * batch
            part = padded[pl.ds(first, rows + 2), :, at : at + cols * batch]
            parts.append(part.reshape((rows + 2) * share, cols * batch))
        left = jnp.concatenate(parts, axis=0)
        right = jnp.concatenate(
            [
                field[row, start : start + cols].reshape(cols * batch, channels)
                for row in range(rows)
            ],
            axis=1,
        )
        total[...] += dot(left, right, FLAT)

    @pl.when(step == pl.num_programs(0) - 1)
    def _():
        for row_tap in range(3):
            for col_tap in range(3):
                value = jnp.zeros((share, channels), jnp.float32)
                for row in range(rows):
                    start = col_tap * (rows + 2) * share + (row + 2 - row_tap) * share
                    value += total[
                        start : start + share, row * channels : (row + 1) * channels
                    ]
                out[row_tap * 3 + col_tap] = value


def filter_terms(turned, field):
    side, _, batch, channels = field.shape
    share = turned.shape[1]
    rows = 2
    return pl.pallas_call(
        filters_kernel,
        grid=(side // rows,),
        in_specs=[
            pl.BlockSpec(memory_space=pl.ANY),
            pl.BlockSpec((rows, side, batch, channels), lambda i: (i, 0, 0, 0)),
        ],
        out_specs=pl.BlockSpec((9, share, channels), lambda i: (0, 0, 0)),
        out_shape=jax.ShapeDtypeStruct((9, share, channels), jnp.float32),
        scratch_shapes=[
            pltpu.VMEM((side + 2, share, (side + 2) * batch), jnp.bfloat16),
            pltpu.VMEM((3 * (rows + 2) * share, rows * channels), jnp.float32),
            pltpu.SemaphoreType.DMA,
        ],
        compiler_params=pltpu.CompilerParams(vmem_limit_bytes=BIG),
        cost_estimate=pl.CostEstimate(
            flops=24 * share * field.size, bytes_accessed=3 * field.size, transcendentals=0
        ),
        name="filters",
    )(turned, field)


def seam_kernel(
    scale, own_turn, east_turn, west_turn, across_turn, field, after, inner,
    east, west, across, out, field_edge, sem,
):
    share = out.shape[1]
    side, batch, channels = field_edge.shape[1:]
    lower = lax.axis_index("tile").astype(jnp.int32) % 2
    turns = (east_turn[0], west_turn[0], across_turn[0])
    fetch_edges(own_turn[0], lower, field, field_edge, sem)
    out[...] = inner[...]
    for edge, message in enumerate((east, west, across)):
        wait_edge(field, field_edge, sem, edge)
        turned = message[2 * share :]
        left = jnp.concatenate([earlier(turned, batch), turned, later(turned, batch)], axis=0)
        terms = dot(left, field_edge[edge].reshape(side * batch, channels), FLAT)
        for d in range(3):
            tap = edge_tap(turns[edge], lower, edge, d, False)
            out[tap] += terms[d * share : (d + 1) * share]
    out[...] = out[...] * scale


def seam_filters(scale, turns, field, after, inner, messages):
    side, _, batch, channels = field.shape
    smem = pl.BlockSpec(memory_space=pltpu.SMEM)
    vmem = pl.BlockSpec(memory_space=pltpu.VMEM)
    anywhere = pl.BlockSpec(memory_space=pl.ANY)

    def body(*refs):
        seam_kernel(scale, *refs)

    return pl.pallas_call(
        body,
        in_specs=[smem] * 4 + [anywhere] * 2 + [vmem] * 4,
        out_specs=vmem,
        out_shape=jax.ShapeDtypeStruct(inner.shape, jnp.float32),
        scratch_shapes=[
            pltpu.VMEM((3, side, batch, channels), jnp.bfloat16),
            pltpu.SemaphoreType.DMA((3,)),
        ],
        compiler_params=pltpu.CompilerParams(vmem_limit_bytes=BIG),
        cost_estimate=pl.CostEstimate(
            flops=18 * inner.shape[1] * side * batch * channels,
            bytes_accessed=6 * side * batch * channels,
            transcendentals=0,
        ),
        name="seam_filters",
    )(*turns, field, after, inner, *messages)


def padded_rows(source, padded, sems):
    side, _, batch, channels = source.shape

    def row_copy(row):
        return pltpu.make_async_copy(
            source.at[row], padded.at[row, pl.ds(1, side)], sems.at[row]
        )

    for row in range(side):
        row_copy(row).start()
    tile = jnp.zeros((batch, channels), padded.dtype)

    @pl.loop(0, side)
    def _(row):
        padded[row, 0] = tile
        padded[row, side + 1] = tile

    return row_copy


def spread_filters(block_of, spread, share, channels):
    empty = jnp.zeros((share, channels), spread.dtype)
    for row in range(3):
        for out_col in range(2):
            for in_col in range(4):
                tap = in_col - out_col
                to = (row * 2 + out_col) * share
                at = in_col * channels
                spread[to : to + share, at : at + channels] = (
                    block_of(row, tap) if 0 <= tap <= 2 else empty
                )


def convolve_rows(row_copy, padded, spread, sums, finished, share):
    side, cols, batch, channels = padded.shape
    cols -= 2

    @pl.loop(0, side)
    def _(row):
        row_copy(row).wait()
        for start in range(0, cols, 4):
            right = jnp.concatenate(
                [
                    jnp.concatenate(
                        [padded[row, start + half + col] for col in range(4)], axis=1
                    )
                    for half in (0, 2)
                ],
                axis=0,
            )
            terms = dot(spread[...], right, TURNED)
            for half in (0, 2):
                for col in range(2):
                    at = start + half + col
                    part = [
                        terms[
                            (k * 2 + col) * share : (k * 2 + col + 1) * share,
                            half // 2 * batch : (half // 2 + 1) * batch,
                        ]
                        for k in range(3)
                    ]
                    sums[row + 2, at] += part[0]
                    sums[row + 1, at] += part[1]
                    finished(row, at, sums[row, at] + part[2])

    for at in range(cols):
        finished(side, at, sums[side, at])


def grad_kernel(weight, other1, other2, other3, source, out, padded, spread, sums, whole, sems):
    side, _, batch, channels = source.shape
    share = weight.shape[1]
    row_copy = padded_rows(source, padded, sems)
    gather_filters((weight, other1, other2, other3), whole)
    pick = one_hot(share, channels)

    def block_of(row, col):
        return dot(pick, whole[8 - row * 3 - col], TURNED).astype(jnp.bfloat16)

    spread_filters(block_of, spread, share, channels)
    sums[...] = jnp.zeros_like(sums)

    def finished(row, col, value):
        out[jnp.maximum(row - 1, 0), col] = value.astype(out.dtype)

    convolve_rows(row_copy, padded, spread, sums, finished, share)


def grad_conv(source, weights):
    side, _, batch, channels = source.shape
    taps, share, _ = weights[0].shape
    vmem = pl.BlockSpec(memory_space=pltpu.VMEM)
    return pl.pallas_call(
        grad_kernel,
        in_specs=[vmem] * len(weights) + [pl.BlockSpec(memory_space=pl.ANY)],
        out_specs=vmem,
        out_shape=jax.ShapeDtypeStruct((side, side, share, batch), jnp.bfloat16),
        scratch_shapes=[
            pltpu.VMEM((side, side + 2, batch, channels), jnp.bfloat16),
            pltpu.VMEM((6 * share, 4 * channels), jnp.bfloat16),
            pltpu.VMEM((side + 2, side, share, batch), jnp.float32),
            pltpu.VMEM((taps, channels, channels), jnp.bfloat16),
            pltpu.SemaphoreType.DMA((side,)),
        ],
        compiler_params=pltpu.CompilerParams(vmem_limit_bytes=BIG),
        cost_estimate=pl.CostEstimate(
            flops=24 * share * source.size, bytes_accessed=3 * source.size, transcendentals=0
        ),
        name="grad_conv",
    )(*weights, source)


def border_pieces(side, source, target, sems):
    inner = pl.ds(1, side - 2)
    return [
        pltpu.make_async_copy(source.at[where], target.at[where], sems.at[index])
        for index, where in enumerate(((0,), (side - 1,), (inner, 0), (inner, side - 1)))
    ]


def conv_kernel(
    own_turn, weight, source, east, west, across, grad_in, out, grad_out,
    padded, spread, sums, grad_held, sems, in_sems, out_sems,
):
    side, _, batch, channels = source.shape
    share = weight.shape[1]
    row_copy = padded_rows(source, padded, sems)
    for copy in border_pieces(side, grad_in, grad_held, in_sems):
        copy.start()

    def block_of(row, col):
        return weight[row * 3 + col]

    spread_filters(block_of, spread, share, channels)
    sums[...] = jnp.zeros_like(sums)
    lower = lax.axis_index("tile").astype(jnp.int32) % 2
    turn = own_turn[0]
    for copy in border_pieces(side, grad_in, grad_held, in_sems):
        copy.wait()
    for edge, message in enumerate((east, west, across)):
        (row, col), (down, right) = edge_place(turn, lower, edge, side)
        for pos in range(side):
            here, there = row + pos * down, col + pos * right
            lanes = slice(pos * batch, (pos + 1) * batch)
            sums[here + 1, there] += message[0:share, lanes].astype(jnp.float32)
            term = message[share : 2 * share, lanes].astype(jnp.float32)
            grad_held[here, there] = (
                grad_held[here, there].astype(jnp.float32) + term
            ).astype(jnp.bfloat16)
    for copy in border_pieces(side, grad_held, grad_out, out_sems):
        copy.start()

    def finished(row, col, value):
        out[jnp.maximum(row - 1, 0), col] = value.astype(out.dtype)

    convolve_rows(row_copy, padded, spread, sums, finished, share)
    for copy in border_pieces(side, grad_held, grad_out, out_sems):
        copy.wait()


def conv_and_borders(turn, weight, source, messages, grad):
    side, _, batch, channels = source.shape
    _, share, _ = weight.shape
    smem = pl.BlockSpec(memory_space=pltpu.SMEM)
    vmem = pl.BlockSpec(memory_space=pltpu.VMEM)
    anywhere = pl.BlockSpec(memory_space=pl.ANY)
    shape = jax.ShapeDtypeStruct((side, side, share, batch), jnp.bfloat16)
    return pl.pallas_call(
        conv_kernel,
        in_specs=[smem, vmem, anywhere] + [vmem] * 3 + [anywhere],
        out_specs=[vmem, anywhere],
        out_shape=[shape, shape],
        scratch_shapes=[
            pltpu.VMEM((side, side + 2, batch, channels), jnp.bfloat16),
            pltpu.VMEM((6 * share, 4 * channels), jnp.bfloat16),
            pltpu.VMEM((side + 2, side, share, batch), jnp.float32),
            pltpu.VMEM((side, side, share, batch), jnp.bfloat16),
            pltpu.SemaphoreType.DMA((side,)),
            pltpu.SemaphoreType.DMA((4,)),
            pltpu.SemaphoreType.DMA((4,)),
        ],
        input_output_aliases={6: 1},
        compiler_params=pltpu.CompilerParams(vmem_limit_bytes=BIG),
        cost_estimate=pl.CostEstimate(
            flops=24 * share * source.size, bytes_accessed=3 * source.size, transcendentals=0
        ),
        name="conv",
    )(turn, weight, source, *messages, grad)


def per_device(tiles, orientation, weight, grad_out):
    field = tiles[0]
    upstream = grad_out[0]
    batch, side, _, channels = field.shape
    share = weight.shape[3]
    count = lax.axis_size("tile")
    eastward = [(i, (i + 2) % count) for i in range(count)]
    westward = [(i, (i - 2) % count) for i in range(count)]
    acrossward = [(i, i ^ 1) for i in range(count)]

    turns = [orientation] + [
        lax.ppermute(orientation, "tile", pairs)
        for pairs in (westward, eastward, acrossward)
    ]
    own = weight.transpose(0, 1, 3, 2).reshape(9, share, channels)
    weights = [own] + [
        lax.ppermute(own, "chan", [(i, i ^ flip) for i in range(channels // share)])
        for flip in range(1, channels // share)
    ]

    field_laid, upstream_laid, turned = relay(field, upstream, share)
    sends = edge_messages(turns, field_laid, upstream_laid, weights)
    from_west = lax.ppermute(sends[0], "tile", eastward)
    from_east = lax.ppermute(sends[1], "tile", westward)
    from_across = lax.ppermute(sends[2], "tile", acrossward)
    messages = (from_east, from_west, from_across)

    inner = filter_terms(turned, field_laid)
    grad = grad_conv(upstream_laid, weights)
    scale = 1.0 / math.sqrt(count * batch * side * side)
    total = seam_filters(scale, turns, field_laid, grad, inner, messages)
    conv, grad = conv_and_borders(orientation, own, field_laid, messages, grad)
    bit = 1
    while bit < count:
        pairs = [(i, i ^ bit) for i in range(count)]
        total = total + lax.ppermute(total, "tile", pairs)
        bit *= 2
    conv_out = conv.transpose(3, 0, 1, 2)[None]
    grad_input = grad.transpose(3, 0, 1, 2)[None]
    grad_weight = total.reshape(3, 3, share, channels).transpose(0, 1, 3, 2)
    return conv_out, grad_input, grad_weight


def solution(mesh):
    in_specs = (
        P("tile", None, None, None, None),
        P("tile"),
        P(None, None, None, "chan"),
        P("tile", None, None, None, None),
    )
    out_specs = (
        P("tile", None, None, None, "chan"),
        P("tile", None, None, None, "chan"),
        P(None, None, None, "chan"),
    )
    return jax.shard_map(
        per_device, mesh=mesh, in_specs=in_specs, out_specs=out_specs, check_vma=False
    )
```

```python
import math

import jax
import jax.numpy as jnp
from jax import lax
from jax.experimental import pallas as pl
from jax.experimental.pallas import tpu as pltpu
from jax.sharding import PartitionSpec as P

BIG = 56 << 20
FLAT = (((1,), (0,)), ((), ()))
TURNED = (((1,), (1,)), ((), ()))


def dot(left, right, dims):
    return lax.dot_general(left, right, dims, preferred_element_type=jnp.float32)


def stored(turn, row, col, last):

    def chosen(values):
        return jnp.where(
            turn < 2,
            jnp.where(turn == 0, values[0], values[1]),
            jnp.where(turn == 2, values[2], values[3]),
        )

    return (
        chosen((row, last - col, last - row, col)),
        chosen((col, row, last - col, last - row)),
    )


def edge_place(turn, lower, edge, side):
    last = side - 1
    if edge == 0:
        start, after = (0, last), (1, last)
    elif edge == 1:
        start, after = (0, 0), (1, 0)
    else:
        row = last * (1 - lower)
        start, after = (row, 0), (row, 1)
    row, col = stored(turn, *start, last)
    below, beside = stored(turn, *after, last)
    first = row * side + col
    return first, below * side + beside - first


def edge_tap(turn, lower, edge, along, outward):
    if edge == 0:
        cell = (along, 2 if outward else 0)
    elif edge == 1:
        cell = (along, 0 if outward else 2)
    else:
        cell = (2 - 2 * lower if outward else 2 * lower, along)
    row, col = stored(turn, *cell, 2)
    return row * 3 + col


def one_hot(share, channels):
    chan = lax.axis_index("chan").astype(jnp.int32)
    rows = lax.broadcasted_iota(jnp.int32, (share, channels), 0) + chan * share
    cols = lax.broadcasted_iota(jnp.int32, (share, channels), 1)
    return jnp.where(rows == cols, 1.0, 0.0).astype(jnp.bfloat16)


def half_of_band():
    return lax.axis_index("tile").astype(jnp.int32) % 2


def later(value, width):
    empty = jnp.zeros((value.shape[0], width), value.dtype)
    return jnp.concatenate([empty, value[:, :-width]], axis=1)


def earlier(value, width):
    empty = jnp.zeros((value.shape[0], width), value.dtype)
    return jnp.concatenate([value[:, width:], empty], axis=1)


def edge_pixels(turn, lower, edge, held, side):
    first, step = edge_place(turn, lower, edge, side)
    return jnp.concatenate([held[first + pos * step] for pos in range(side)], axis=0)


def terms_of(product, share, batch):
    return (
        later(product[:share], batch)
        + product[share : 2 * share]
        + earlier(product[2 * share : 3 * share], batch)
    ).astype(jnp.bfloat16)


def gather_filters(parts, whole):
    taps, share, _ = parts[0].shape
    chan = lax.axis_index("chan").astype(jnp.int32)
    for flip, part in enumerate(parts):
        start = pl.multiple_of((chan ^ flip) * share, share)
        for tap in range(taps):
            whole[tap, pl.ds(start, share)] = part[tap]


def pair_in(source, stage, sems, pair):
    return pltpu.make_async_copy(
        source.at[:, pl.ds(2 * pair, 2)], stage.at[pair], sems.at[pair]
    )


def pair_out(held, laid, sems, pair, side):
    pixels = pl.ds(2 * pair * side, 2 * side)
    return pltpu.make_async_copy(held.at[pixels], laid.at[pixels], sems.at[pair])


def upstream_kernel(
    own_turn, weight, other1, other2, other3, upstream,
    laid, turned, east, west, across,
    stage, held, flat, whole, rowed, shuffle, in_sems, out_sems, turned_sems,
):
    pairs, batch, rows, side, channels = stage.shape
    taps, share, _ = weight.shape
    group = 256 // side
    for pair in range(pairs):
        pair_in(upstream, stage, in_sems, pair).start()
    to = lax.broadcasted_iota(jnp.int32, (256, 256), 0)
    come = lax.broadcasted_iota(jnp.int32, (256, 256), 1)
    same = (to // group == come % side) & (to % group == come // side)
    shuffle[...] = jnp.where(same, 1.0, 0.0).astype(jnp.bfloat16)
    pick = one_hot(share, channels)
    gather_filters((weight, other1, other2, other3), whole)
    for tap in range(taps):
        rowed[tap] = dot(pick, whole[tap], TURNED).astype(jnp.bfloat16)

    def turned_out(pair):
        part = pl.ds(2 * pair, 2)
        return pltpu.make_async_copy(flat.at[part], turned.at[part], turned_sems.at[pair])

    @pl.loop(0, pairs)
    def _(pair):
        pair_in(upstream, stage, in_sems, pair).wait()
        for start in range(0, batch, group):
            block = jnp.concatenate(
                [
                    stage[pair, start : start + group, row].reshape(256, channels)
                    for row in range(rows)
                ],
                axis=1,
            )
            moved = dot(shuffle[...], block, FLAT).astype(jnp.bfloat16)
            for row in range(rows):
                pixels = pl.ds((2 * pair + row) * side, side)
                held[pixels, start : start + group] = moved[
                    :, row * channels : (row + 1) * channels
                ].reshape(side, group, channels)
        pair_out(held, laid, out_sems, pair, side).start()
        for row in range(rows):
            pixels = pl.ds((2 * pair + row) * side, side)
            flat[2 * pair + row] = dot(
                pick, held[pixels].reshape(side * batch, channels), TURNED
            ).astype(jnp.bfloat16)
        turned_out(pair).start()

    lower = half_of_band()
    turn = own_turn[0]
    for edge, out in enumerate((east, west, across)):
        filters = jnp.concatenate(
            [rowed[edge_tap(turn, lower, edge, 2 - d, True)] for d in range(3)] + [pick],
            axis=0,
        )
        product = dot(filters, edge_pixels(turn, lower, edge, held, side), TURNED)
        out[0:share] = terms_of(product, share, batch)
        out[share:] = product[3 * share :].astype(jnp.bfloat16)
    for pair in range(pairs):
        pair_out(held, laid, out_sems, pair, side).wait()
        turned_out(pair).wait()


def lay_upstream(turn, weights, upstream):
    batch, side, _, channels = upstream.shape
    taps, share, _ = weights[0].shape
    smem = pl.BlockSpec(memory_space=pltpu.SMEM)
    vmem = pl.BlockSpec(memory_space=pltpu.VMEM)
    anywhere = pl.BlockSpec(memory_space=pl.ANY)
    pairs = side // 2
    laid = jax.ShapeDtypeStruct((side * side, batch, channels), jnp.bfloat16)
    turned = jax.ShapeDtypeStruct((side, share, side * batch), jnp.bfloat16)
    message = jax.ShapeDtypeStruct((2 * share, side * batch), jnp.bfloat16)
    return pl.pallas_call(
        upstream_kernel,
        in_specs=[smem] + [vmem] * len(weights) + [anywhere],
        out_specs=[anywhere] * 2 + [vmem] * 3,
        out_shape=[laid, turned] + [message] * 3,
        scratch_shapes=[
            pltpu.VMEM((pairs, batch, 2, side, channels), jnp.bfloat16),
            pltpu.VMEM(laid.shape, jnp.bfloat16),
            pltpu.VMEM(turned.shape, jnp.bfloat16),
            pltpu.VMEM((taps, channels, channels), jnp.bfloat16),
            pltpu.VMEM((taps, share, channels), jnp.bfloat16),
            pltpu.VMEM((256, 256), jnp.bfloat16),
            pltpu.SemaphoreType.DMA((pairs,)),
            pltpu.SemaphoreType.DMA((pairs,)),
            pltpu.SemaphoreType.DMA((pairs,)),
        ],
        compiler_params=pltpu.CompilerParams(vmem_limit_bytes=BIG),
        cost_estimate=pl.CostEstimate(
            flops=1024 * upstream.size, bytes_accessed=5 * upstream.size, transcendentals=0
        ),
        name="lay_upstream",
    )(turn, *weights, upstream)


def field_kernel(
    own_turn, east_turn, west_turn, across_turn, weight, field, turned,
    laid, edges, inner, east, west, across,
    stage, held, padded, total, in_sems, out_sems, turned_sem, edge_sems,
):
    pairs, batch, rows, side, channels = stage.shape
    taps, share, _ = weight.shape
    width = side * batch
    turned_in = pltpu.make_async_copy(
        turned, padded.at[pl.ds(1, side), :, pl.ds(batch, width)], turned_sem
    )
    pair_in(field, stage, in_sems, 0).start()
    turned_in.start()
    for pair in range(1, pairs):
        pair_in(field, stage, in_sems, pair).start()
    padded[0] = jnp.zeros(padded.shape[1:], padded.dtype)
    padded[side + 1] = jnp.zeros(padded.shape[1:], padded.dtype)
    column = jnp.zeros((side, share, batch), padded.dtype)
    padded[1 : side + 1, :, 0:batch] = column
    padded[1 : side + 1, :, width + batch :] = column
    total[...] = jnp.zeros_like(total)

    def lay(pair):
        pair_in(field, stage, in_sems, pair).wait()
        for row in range(rows):
            held[pl.ds((2 * pair + row) * side, side)] = jnp.swapaxes(stage[pair, :, row], 0, 1)
        pair_out(held, laid, out_sems, pair, side).start()

    def add_filters(pair):
        cols = 4
        for start in range(0, side, cols):
            parts = []
            for tap in range(3):
                at = (start + 2 - tap) * batch
                part = padded[pl.ds(2 * pair, rows + 2), :, at : at + cols * batch]
                parts.append(part.reshape((rows + 2) * share, cols * batch))
            left = jnp.concatenate(parts, axis=0)
            right = jnp.concatenate(
                [
                    held[pl.ds((2 * pair + row) * side + start, cols)].reshape(
                        cols * batch, channels
                    )
                    for row in range(rows)
                ],
                axis=1,
            )
            total[...] += dot(left, right, FLAT)

    lay(0)
    turned_in.wait()

    @pl.loop(1, pairs)
    def _(pair):
        add_filters(pair - 1)
        lay(pair)

    lower = half_of_band()
    turn = own_turn[0]
    for edge in range(3):
        first, step = edge_place(turn, lower, edge, side)
        for pos in range(side):
            pltpu.make_async_copy(
                held.at[first + pos * step], edges.at[edge, pos], edge_sems.at[edge]
            ).start()
    turns = (east_turn[0], west_turn[0], across_turn[0])
    for edge, out in enumerate((east, west, across)):
        filters = jnp.concatenate(
            [weight[edge_tap(turns[edge], lower, edge, d, False)] for d in range(3)], axis=0
        )
        product = dot(filters, edge_pixels(turn, lower, edge, held, side), TURNED)
        out[...] = terms_of(product, share, batch)
    add_filters(pairs - 1)
    for row_tap in range(3):
        for col_tap in range(3):
            value = jnp.zeros((share, channels), jnp.float32)
            for row in range(rows):
                start = col_tap * (rows + 2) * share + (row + 2 - row_tap) * share
                value += total[start : start + share, row * channels : (row + 1) * channels]
            inner[row_tap * 3 + col_tap] = value
    for pair in range(pairs):
        pair_out(held, laid, out_sems, pair, side).wait()
    for edge in range(3):
        pltpu.make_async_copy(
            held.at[pl.ds(0, side)], edges.at[edge], edge_sems.at[edge]
        ).wait()


def lay_field(turns, weight, field, turned):
    batch, side, _, channels = field.shape
    taps, share, _ = weight.shape
    smem = pl.BlockSpec(memory_space=pltpu.SMEM)
    vmem = pl.BlockSpec(memory_space=pltpu.VMEM)
    anywhere = pl.BlockSpec(memory_space=pl.ANY)
    pairs = side // 2
    laid = jax.ShapeDtypeStruct((side * side, batch, channels), jnp.bfloat16)
    edges = jax.ShapeDtypeStruct((3, side, batch, channels), jnp.bfloat16)
    inner = jax.ShapeDtypeStruct((taps, share, channels), jnp.float32)
    message = jax.ShapeDtypeStruct((share, side * batch), jnp.bfloat16)
    return pl.pallas_call(
        field_kernel,
        in_specs=[smem] * 4 + [vmem] + [anywhere] * 2,
        out_specs=[anywhere] * 2 + [vmem] * 4,
        out_shape=[laid, edges, inner] + [message] * 3,
        scratch_shapes=[
            pltpu.VMEM((pairs, batch, 2, side, channels), jnp.bfloat16),
            pltpu.VMEM(laid.shape, jnp.bfloat16),
            pltpu.VMEM((side + 2, share, (side + 2) * batch), jnp.bfloat16),
            pltpu.VMEM((12 * share, 2 * channels), jnp.float32),
            pltpu.SemaphoreType.DMA((pairs,)),
            pltpu.SemaphoreType.DMA((pairs,)),
            pltpu.SemaphoreType.DMA,
            pltpu.SemaphoreType.DMA((3,)),
        ],
        compiler_params=pltpu.CompilerParams(vmem_limit_bytes=BIG),
        cost_estimate=pl.CostEstimate(
            flops=1800 * field.size, bytes_accessed=5 * field.size, transcendentals=0
        ),
        name="lay_field",
    )(*turns, weight, field, turned)


def seam_kernel(
    scale, east_turn, west_turn, across_turn, edges, inner, east, west, across, out
):
    side, batch, channels = edges.shape[1:]
    share = out.shape[1]
    lower = half_of_band()
    turns = (east_turn[0], west_turn[0], across_turn[0])
    out[...] = inner[...]
    for edge, message in enumerate((east, west, across)):
        turned = message[share:]
        left = jnp.concatenate([earlier(turned, batch), turned, later(turned, batch)], axis=0)
        terms = dot(left, edges[edge].reshape(side * batch, channels), FLAT)
        for d in range(3):
            tap = edge_tap(turns[edge], lower, edge, d, False)
            out[tap] += terms[d * share : (d + 1) * share]
    out[...] = out[...] * scale


def seam_filters(scale, turns, edges, inner, messages):
    _, side, batch, channels = edges.shape
    share = inner.shape[1]
    smem = pl.BlockSpec(memory_space=pltpu.SMEM)
    vmem = pl.BlockSpec(memory_space=pltpu.VMEM)

    def body(*refs):
        seam_kernel(scale, *refs)

    return pl.pallas_call(
        body,
        in_specs=[smem] * 3 + [vmem] * 5,
        out_specs=vmem,
        out_shape=jax.ShapeDtypeStruct(inner.shape, jnp.float32),
        compiler_params=pltpu.CompilerParams(vmem_limit_bytes=BIG),
        cost_estimate=pl.CostEstimate(
            flops=18 * share * side * batch * channels,
            bytes_accessed=6 * side * batch * channels,
            transcendentals=0,
        ),
        name="seam_filters",
    )(*turns[1:], edges, inner, *messages)


def conv_kernel(mirrored, own_turn, east, west, across, source, *refs):
    out, padded, spread, sums, whole, sems = refs[-6:]
    weights = refs[:-6]
    side, cols, batch, channels = padded.shape
    cols -= 2
    share = weights[0].shape[1]

    def row_copy(row):
        return pltpu.make_async_copy(
            source.at[pl.ds(row * cols, cols)], padded.at[row, pl.ds(1, cols)], sems.at[row]
        )

    for row in range(side):
        row_copy(row).start()
    tile = jnp.zeros((batch, channels), padded.dtype)
    for row in range(side):
        padded[row, 0] = tile
        padded[row, cols + 1] = tile

    if mirrored:
        gather_filters(weights, whole)
        pick = one_hot(share, channels)
    empty = jnp.zeros((share, channels), spread.dtype)
    blocks = [
        dot(pick, whole[8 - tap], TURNED).astype(jnp.bfloat16) if mirrored else weights[0][tap]
        for tap in range(9)
    ]
    for row in range(3):
        for out_col in range(2):
            for in_col in range(4):
                tap = in_col - out_col
                to = (row * 2 + out_col) * share
                at = in_col * channels
                spread[to : to + share, at : at + channels] = (
                    blocks[row * 3 + tap] if 0 <= tap <= 2 else empty
                )
    sums[...] = jnp.zeros_like(sums)
    lower = half_of_band()
    for edge, message in enumerate((east, west, across)):
        first, step = edge_place(own_turn[0], lower, edge, side)
        for pos in range(side):
            sums[first + pos * step + cols] += message[
                0:share, pos * batch : (pos + 1) * batch
            ].astype(jnp.float32)

    @pl.loop(0, side, unroll=4)
    def _(row):
        row_copy(row).wait()
        for start in range(0, cols, 4):
            right = jnp.concatenate(
                [
                    jnp.concatenate(
                        [padded[row, start + half + col] for col in range(4)], axis=1
                    )
                    for half in (0, 2)
                ],
                axis=0,
            )
            terms = dot(spread[...], right, TURNED)
            for half in (0, 2):
                for col in range(2):
                    at = start + half + col
                    part = [
                        terms[
                            (k * 2 + col) * share : (k * 2 + col + 1) * share,
                            half // 2 * batch : (half // 2 + 1) * batch,
                        ]
                        for k in range(3)
                    ]
                    pixel = row * cols + at
                    sums[pixel + 2 * cols] += part[0]
                    sums[pixel + cols] += part[1]
                    done = jnp.maximum(pixel - cols, at)
                    out[done] = (sums[pixel] + part[2]).astype(out.dtype)

    for at in range(cols):
        out[(side - 1) * cols + at] = sums[side * cols + at].astype(out.dtype)


def convolved(mirrored, turn, messages, source, weights, *after):
    pixels, batch, channels = source.shape
    taps, share, _ = weights[0].shape
    side = math.isqrt(pixels)
    smem = pl.BlockSpec(memory_space=pltpu.SMEM)
    vmem = pl.BlockSpec(memory_space=pltpu.VMEM)

    def body(*refs):
        conv_kernel(mirrored, *refs)

    return pl.pallas_call(
        body,
        in_specs=[smem] + [vmem] * 3
        + [pl.BlockSpec(memory_space=pl.ANY)]
        + [vmem] * len(weights)
        + [pl.BlockSpec(memory_space=pl.ANY)] * len(after),
        out_specs=vmem,
        out_shape=jax.ShapeDtypeStruct((pixels, share, batch), jnp.bfloat16),
        scratch_shapes=[
            pltpu.VMEM((side, side + 2, batch, channels), jnp.bfloat16),
            pltpu.VMEM((6 * share, 4 * channels), jnp.bfloat16),
            pltpu.VMEM((pixels + 2 * side, share, batch), jnp.float32),
            pltpu.VMEM((taps, channels, channels), jnp.bfloat16),
            pltpu.SemaphoreType.DMA((side,)),
        ],
        compiler_params=pltpu.CompilerParams(vmem_limit_bytes=BIG),
        cost_estimate=pl.CostEstimate(
            flops=2400 * source.size, bytes_accessed=3 * source.size, transcendentals=0
        ),
        name="grad_conv" if mirrored else "conv",
    )(turn, *messages, source, *weights, *after)


def sum_over_tiles(total, count):
    bit = 1
    while bit < count:
        left = count // bit

        def other(flip):
            return lax.ppermute(total, "tile", [(i, i ^ flip) for i in range(count)])

        if left % 4 == 0 and left.bit_length() % 2 == 1:
            near, far, farther = other(bit), other(2 * bit), other(3 * bit)
            total = (total + near) + (far + farther)
            bit *= 4
        else:
            total = total + other(bit)
            bit *= 2
    return total


def per_device(tiles, orientation, weight, grad_out):
    batch, side, _, channels = tiles.shape[1:]
    share = weight.shape[3]
    count = lax.axis_size("tile")
    eastward = [(i, (i + 2) % count) for i in range(count)]
    westward = [(i, (i - 2) % count) for i in range(count)]
    acrossward = [(i, i ^ 1) for i in range(count)]

    def exchanged(sends):
        return [
            lax.ppermute(sends[1], "tile", westward),
            lax.ppermute(sends[0], "tile", eastward),
            lax.ppermute(sends[2], "tile", acrossward),
        ]

    own = weight.transpose(0, 1, 3, 2).reshape(9, share, channels)
    weights = [own] + [
        lax.ppermute(own, "chan", [(i, i ^ flip) for i in range(channels // share)])
        for flip in range(1, channels // share)
    ]
    turns = [orientation] + [
        lax.ppermute(orientation, "tile", pairs)
        for pairs in (westward, eastward, acrossward)
    ]
    upstream, turned, *sends = lay_upstream(orientation, weights, grad_out[0])
    grad_messages = exchanged(sends)
    field, edges, inner, *sends = lay_field(turns, own, tiles[0], turned)
    conv_messages = exchanged(sends)
    scale = 1.0 / math.sqrt(count * batch * side * side)
    total = seam_filters(scale, turns, edges, inner, grad_messages)
    grad = convolved(True, orientation, grad_messages, upstream, weights)
    conv = convolved(False, orientation, conv_messages, field, weights[:1], grad)
    total = sum_over_tiles(total, count)
    shape = (side, side, share, batch)
    conv_out = conv.reshape(shape).transpose(3, 0, 1, 2)[None]
    grad_input = grad.reshape(shape).transpose(3, 0, 1, 2)[None]
    grad_weight = total.reshape(3, 3, share, channels).transpose(0, 1, 3, 2)
    return conv_out, grad_input, grad_weight


def solution(mesh):
    in_specs = (
        P("tile", None, None, None, None),
        P("tile"),
        P(None, None, None, "chan"),
        P("tile", None, None, None, None),
    )
    out_specs = (
        P("tile", None, None, None, "chan"),
        P("tile", None, None, None, "chan"),
        P(None, None, None, "chan"),
    )
    return jax.shard_map(
        per_device, mesh=mesh, in_specs=in_specs, out_specs=out_specs, check_vma=False
    )
```

```python
import math

import jax
import jax.numpy as jnp
from jax import lax
from jax.experimental import pallas as pl
from jax.experimental.pallas import tpu as pltpu
from jax.sharding import PartitionSpec as P

BIG = 56 << 20
AHEAD = 2
EXTRA = 128
FLAT = (((1,), (0,)), ((), ()))
TURNED = (((1,), (1,)), ((), ()))


def dot(left, right, dims):
    return lax.dot_general(left, right, dims, preferred_element_type=jnp.float32)


def stored(turn, row, col, last):

    def chosen(values):
        return jnp.where(
            turn < 2,
            jnp.where(turn == 0, values[0], values[1]),
            jnp.where(turn == 2, values[2], values[3]),
        )

    return (
        chosen((row, last - col, last - row, col)),
        chosen((col, row, last - col, last - row)),
    )


def edge_place(turn, lower, edge, side):
    last = side - 1
    if edge == 0:
        start, after = (0, last), (1, last)
    elif edge == 1:
        start, after = (0, 0), (1, 0)
    else:
        row = last * (1 - lower)
        start, after = (row, 0), (row, 1)
    row, col = stored(turn, *start, last)
    below, beside = stored(turn, *after, last)
    first = row * side + col
    return first, below * side + beside - first


def edge_tap(turn, lower, edge, along, outward):
    if edge == 0:
        cell = (along, 2 if outward else 0)
    elif edge == 1:
        cell = (along, 0 if outward else 2)
    else:
        cell = (2 - 2 * lower if outward else 2 * lower, along)
    row, col = stored(turn, *cell, 2)
    return row * 3 + col


def one_hot(share, channels):
    chan = lax.axis_index("chan").astype(jnp.int32)
    rows = lax.broadcasted_iota(jnp.int32, (share, channels), 0) + chan * share
    cols = lax.broadcasted_iota(jnp.int32, (share, channels), 1)
    return jnp.where(rows == cols, 1.0, 0.0).astype(jnp.bfloat16)


def half_of_band():
    return lax.axis_index("tile").astype(jnp.int32) % 2


def later(value, width):
    empty = jnp.zeros((value.shape[0], width), value.dtype)
    return jnp.concatenate([empty, value[:, :-width]], axis=1)


def earlier(value, width):
    empty = jnp.zeros((value.shape[0], width), value.dtype)
    return jnp.concatenate([value[:, width:], empty], axis=1)


def edge_pixels(turn, lower, edge, held, side):
    first, step = edge_place(turn, lower, edge, side)
    return jnp.concatenate([held[first + pos * step] for pos in range(side)], axis=0)


def terms_of(product, share, batch):
    return (
        later(product[:share], batch)
        + product[share : 2 * share]
        + earlier(product[2 * share : 3 * share], batch)
    ).astype(jnp.bfloat16)


def gather_filters(parts, whole):
    taps, share, _ = parts[0].shape
    chan = lax.axis_index("chan").astype(jnp.int32)
    for flip, part in enumerate(parts):
        start = pl.multiple_of((chan ^ flip) * share, share)
        for tap in range(taps):
            whole[tap, pl.ds(start, share)] = part[tap]


def pair_in(source, stage, sems, pair):
    return pltpu.make_async_copy(
        source.at[:, pl.ds(2 * pair, 2)], stage.at[pair], sems.at[pair]
    )


def pair_out(held, laid, sems, pair, side):
    pixels = pl.ds(2 * pair * side, 2 * side)
    return pltpu.make_async_copy(held.at[pixels], laid.at[pixels], sems.at[pair])


def upstream_kernel(
    own_turn, weight, other1, other2, other3, upstream,
    laid, turned, east, west, across,
    stage, held, flat, whole, rowed, shuffle, in_sems, out_sems, turned_sems,
):
    pairs, batch, rows, side, channels = stage.shape
    taps, share, _ = weight.shape
    group = 256 // side
    for pair in range(AHEAD):
        pair_in(upstream, stage, in_sems, pair).start()
    to = lax.broadcasted_iota(jnp.int32, (256, 256), 0)
    come = lax.broadcasted_iota(jnp.int32, (256, 256), 1)
    same = (to // group == come % side) & (to % group == come // side)
    shuffle[...] = jnp.where(same, 1.0, 0.0).astype(jnp.bfloat16)
    pick = one_hot(share, channels)
    gather_filters((weight, other1, other2, other3), whole)
    for tap in range(taps):
        rowed[tap] = dot(pick, whole[tap], TURNED).astype(jnp.bfloat16)

    def turned_out(pair):
        part = pl.ds(2 * pair, 2)
        return pltpu.make_async_copy(flat.at[part], turned.at[part], turned_sems.at[pair])

    @pl.loop(0, pairs)
    def _(pair):
        @pl.when(pair + AHEAD < pairs)
        def _():
            pair_in(upstream, stage, in_sems, pair + AHEAD).start()

        pair_in(upstream, stage, in_sems, pair).wait()
        for start in range(0, batch, group):
            block = jnp.concatenate(
                [
                    stage[pair, start : start + group, row].reshape(256, channels)
                    for row in range(rows)
                ],
                axis=1,
            )
            moved = dot(shuffle[...], block, FLAT).astype(jnp.bfloat16)
            for row in range(rows):
                pixels = pl.ds((2 * pair + row) * side, side)
                held[pixels, start : start + group] = moved[
                    :, row * channels : (row + 1) * channels
                ].reshape(side, group, channels)
        pair_out(held, laid, out_sems, pair, side).start()
        for row in range(rows):
            pixels = pl.ds((2 * pair + row) * side, side)
            flat[2 * pair + row] = dot(
                pick, held[pixels].reshape(side * batch, channels), TURNED
            ).astype(jnp.bfloat16)
        turned_out(pair).start()

    lower = half_of_band()
    turn = own_turn[0]
    for edge, out in enumerate((east, west, across)):
        filters = jnp.concatenate(
            [rowed[edge_tap(turn, lower, edge, 2 - d, True)] for d in range(3)] + [pick],
            axis=0,
        )
        product = dot(filters, edge_pixels(turn, lower, edge, held, side), TURNED)
        out[0:share, 0 : side * batch] = terms_of(product, share, batch)
        out[share:, 0 : side * batch] = product[3 * share :].astype(jnp.bfloat16)
        code = jnp.full((2 * share, EXTRA), turn, jnp.int32)
        out[:, side * batch :] = code.astype(jnp.float32).astype(jnp.bfloat16)
    for pair in range(pairs):
        pair_out(held, laid, out_sems, pair, side).wait()
        turned_out(pair).wait()


def lay_upstream(turn, weights, upstream):
    batch, side, _, channels = upstream.shape
    taps, share, _ = weights[0].shape
    smem = pl.BlockSpec(memory_space=pltpu.SMEM)
    vmem = pl.BlockSpec(memory_space=pltpu.VMEM)
    anywhere = pl.BlockSpec(memory_space=pl.ANY)
    pairs = side // 2
    laid = jax.ShapeDtypeStruct((side * side, batch, channels), jnp.bfloat16)
    turned = jax.ShapeDtypeStruct((side, share, side * batch), jnp.bfloat16)
    message = jax.ShapeDtypeStruct((2 * share, side * batch + EXTRA), jnp.bfloat16)
    return pl.pallas_call(
        upstream_kernel,
        in_specs=[smem] + [vmem] * len(weights) + [anywhere],
        out_specs=[anywhere] * 2 + [vmem] * 3,
        out_shape=[laid, turned] + [message] * 3,
        scratch_shapes=[
            pltpu.VMEM((pairs, batch, 2, side, channels), jnp.bfloat16),
            pltpu.VMEM(laid.shape, jnp.bfloat16),
            pltpu.VMEM(turned.shape, jnp.bfloat16),
            pltpu.VMEM((taps, channels, channels), jnp.bfloat16),
            pltpu.VMEM((taps, share, channels), jnp.bfloat16),
            pltpu.VMEM((256, 256), jnp.bfloat16),
            pltpu.SemaphoreType.DMA((pairs,)),
            pltpu.SemaphoreType.DMA((pairs,)),
            pltpu.SemaphoreType.DMA((pairs,)),
        ],
        compiler_params=pltpu.CompilerParams(vmem_limit_bytes=BIG),
        cost_estimate=pl.CostEstimate(
            flops=1024 * upstream.size, bytes_accessed=5 * upstream.size, transcendentals=0
        ),
        name="lay_upstream",
    )(turn, *weights, upstream)


def field_kernel(
    own_turn, field, turned, laid, edges, inner,
    stage, held, padded, total, in_sems, out_sems, turned_sem, edge_sems,
):
    pairs, batch, rows, side, channels = stage.shape
    share = padded.shape[1]
    width = side * batch
    turned_in = pltpu.make_async_copy(
        turned, padded.at[pl.ds(1, side), :, pl.ds(batch, width)], turned_sem
    )
    pair_in(field, stage, in_sems, 0).start()
    turned_in.start()
    for pair in range(1, AHEAD):
        pair_in(field, stage, in_sems, pair).start()
    padded[0] = jnp.zeros(padded.shape[1:], padded.dtype)
    padded[side + 1] = jnp.zeros(padded.shape[1:], padded.dtype)
    column = jnp.zeros((side, share, batch), padded.dtype)
    padded[1 : side + 1, :, 0:batch] = column
    padded[1 : side + 1, :, width + batch :] = column
    total[...] = jnp.zeros_like(total)

    def lay(pair):
        pair_in(field, stage, in_sems, pair).wait()
        for row in range(rows):
            held[pl.ds((2 * pair + row) * side, side)] = jnp.swapaxes(stage[pair, :, row], 0, 1)
        pair_out(held, laid, out_sems, pair, side).start()

    def add_filters(pair):
        cols = 8
        for start in range(0, side, cols):
            right = jnp.concatenate(
                [
                    held[pl.ds((2 * pair + row) * side + start, cols)].reshape(
                        cols * batch, channels
                    )
                    for row in range(rows)
                ],
                axis=1,
            )
            parts = []
            for tap in range(3):
                at = (start + 2 - tap) * batch
                for half in range(2):
                    part = padded[pl.ds(2 * pair + 2 * half, 2), :, at : at + cols * batch]
                    parts.append(part.reshape(2 * share, cols * batch))
            for half in range(2):
                left = jnp.concatenate(parts[3 * half : 3 * half + 3], axis=0)
                total[6 * share * half : 6 * share * (half + 1)] += dot(left, right, FLAT)

    lay(0)
    turned_in.wait()

    @pl.loop(1, pairs)
    def _(pair):
        @pl.when(pair + AHEAD - 1 < pairs)
        def _():
            pair_in(field, stage, in_sems, pair + AHEAD - 1).start()

        add_filters(pair - 1)
        lay(pair)

    lower = half_of_band()
    turn = own_turn[0]
    for edge in range(3):
        first, step = edge_place(turn, lower, edge, side)
        for pos in range(side):
            pltpu.make_async_copy(
                held.at[first + pos * step], edges.at[edge, pos], edge_sems.at[edge]
            ).start()
    add_filters(pairs - 1)
    for row_tap in range(3):
        for col_tap in range(3):
            value = jnp.zeros((share, channels), jnp.float32)
            for row in range(rows):
                start = col_tap * (rows + 2) * share + (row + 2 - row_tap) * share
                value += total[start : start + share, row * channels : (row + 1) * channels]
            inner[row_tap * 3 + col_tap] = value
    for pair in range(pairs):
        pair_out(held, laid, out_sems, pair, side).wait()
    for edge in range(3):
        pltpu.make_async_copy(
            held.at[pl.ds(0, side)], edges.at[edge], edge_sems.at[edge]
        ).wait()


def lay_field(turn, field, turned):
    batch, side, _, channels = field.shape
    share = turned.shape[1]
    anywhere = pl.BlockSpec(memory_space=pl.ANY)
    pairs = side // 2
    laid = jax.ShapeDtypeStruct((side * side, batch, channels), jnp.bfloat16)
    edges = jax.ShapeDtypeStruct((3, side, batch, channels), jnp.bfloat16)
    inner = jax.ShapeDtypeStruct((9, share, channels), jnp.float32)
    return pl.pallas_call(
        field_kernel,
        in_specs=[pl.BlockSpec(memory_space=pltpu.SMEM)] + [anywhere] * 2,
        out_specs=[anywhere] * 2 + [pl.BlockSpec(memory_space=pltpu.VMEM)],
        out_shape=[laid, edges, inner],
        scratch_shapes=[
            pltpu.VMEM((pairs, batch, 2, side, channels), jnp.bfloat16),
            pltpu.VMEM(laid.shape, jnp.bfloat16),
            pltpu.VMEM((side + 2, share, (side + 2) * batch), jnp.bfloat16),
            pltpu.VMEM((12 * share, 2 * channels), jnp.float32),
            pltpu.SemaphoreType.DMA((pairs,)),
            pltpu.SemaphoreType.DMA((pairs,)),
            pltpu.SemaphoreType.DMA,
            pltpu.SemaphoreType.DMA((3,)),
        ],
        compiler_params=pltpu.CompilerParams(vmem_limit_bytes=BIG),
        cost_estimate=pl.CostEstimate(
            flops=1800 * field.size, bytes_accessed=5 * field.size, transcendentals=0
        ),
        name="lay_field",
    )(turn, field, turned)


def seam_kernel(scale, edges, inner, weight, *refs):
    messages, out, terms_out = refs[:3], refs[3], refs[4:7]
    side, batch, channels = edges.shape[1:]
    share = out.shape[1]
    width = side * batch
    lower = half_of_band()
    out[...] = inner[...]
    for edge, message in enumerate(messages):
        turn = jnp.max(message[0:16, width:].astype(jnp.float32)).astype(jnp.int32)
        taps = [edge_tap(turn, lower, edge, d, False) for d in range(3)]
        turned = message[share:, 0:width]
        left = jnp.concatenate([earlier(turned, batch), turned, later(turned, batch)], axis=0)
        pixels = edges[edge].reshape(width, channels)
        terms = dot(left, pixels, FLAT)
        for d in range(3):
            out[taps[d]] += terms[d * share : (d + 1) * share]
        filters = jnp.concatenate([weight[tap] for tap in taps], axis=0)
        terms_out[edge][...] = terms_of(dot(filters, pixels, TURNED), share, batch)
    out[...] = out[...] * scale


def seam_filters(scale, edges, inner, weight, messages):
    _, side, batch, channels = edges.shape
    share = inner.shape[1]
    vmem = pl.BlockSpec(memory_space=pltpu.VMEM)

    def body(*refs):
        seam_kernel(scale, *refs)

    return pl.pallas_call(
        body,
        in_specs=[vmem] * 6,
        out_specs=[vmem] * 4,
        out_shape=[jax.ShapeDtypeStruct(inner.shape, jnp.float32)]
        + [jax.ShapeDtypeStruct((share, side * batch), jnp.bfloat16)] * 3,
        compiler_params=pltpu.CompilerParams(vmem_limit_bytes=BIG),
        cost_estimate=pl.CostEstimate(
            flops=36 * share * side * batch * channels,
            bytes_accessed=6 * side * batch * channels,
            transcendentals=0,
        ),
        name="seam_filters",
    )(edges, inner, weight, *messages)


def add_messages(turn, messages, sums, offset, share, batch, side):
    lower = half_of_band()
    for edge, message in enumerate(messages):
        first, step = edge_place(turn, lower, edge, side)
        for pos in range(side):
            sums[first + pos * step + offset] += message[
                0:share, pos * batch : (pos + 1) * batch
            ].astype(jnp.float32)


def grad_kernel(own_turn, east, west, across, source, *refs):
    out, padded, spread, sums, done, whole, sems, out_sems = refs[-8:]
    weights = refs[:-8]
    side, cols, batch, channels = padded.shape
    cols -= 2
    share = weights[0].shape[1]
    ahead = 3

    def row_copy(row):
        return pltpu.make_async_copy(
            source.at[pl.ds(row * cols, cols)], padded.at[row, pl.ds(1, cols)], sems.at[row]
        )

    def row_out(row):
        pixels = pl.ds(row * cols, cols)
        return pltpu.make_async_copy(done.at[pixels], out.at[pixels], out_sems.at[row])

    for row in range(ahead):
        row_copy(row).start()
    tile = jnp.zeros((batch, channels), padded.dtype)
    for row in range(side):
        padded[row, 0] = tile
        padded[row, cols + 1] = tile

    gather_filters(weights, whole)
    pick = one_hot(share, channels)
    empty = jnp.zeros((share, channels), spread.dtype)
    blocks = [dot(pick, whole[8 - tap], TURNED).astype(jnp.bfloat16) for tap in range(9)]
    for row in range(3):
        for out_col in range(2):
            for in_col in range(4):
                tap = in_col - out_col
                to = (row * 2 + out_col) * share
                at = in_col * channels
                spread[to : to + share, at : at + channels] = (
                    blocks[row * 3 + tap] if 0 <= tap <= 2 else empty
                )
    sums[...] = jnp.zeros_like(sums)
    add_messages(own_turn[0], (east, west, across), sums, cols, share, batch, side)

    def add_row(row):
        for start in range(0, cols, 4):
            right = jnp.concatenate(
                [
                    jnp.concatenate(
                        [padded[row, start + half + col] for col in range(4)], axis=1
                    )
                    for half in (0, 2)
                ],
                axis=0,
            )
            terms = dot(spread[...], right, TURNED)
            for half in (0, 2):
                for col in range(2):
                    part = [
                        terms[
                            (k * 2 + col) * share : (k * 2 + col + 1) * share,
                            half // 2 * batch : (half // 2 + 1) * batch,
                        ]
                        for k in range(3)
                    ]
                    at = start + half + col
                    pixel = row * cols + at
                    sums[pixel + 2 * cols] += part[0]
                    sums[pixel + cols] += part[1]
                    done[jnp.maximum(pixel - cols, at)] = (sums[pixel] + part[2]).astype(
                        done.dtype
                    )

    row_copy(0).wait()
    row_copy(ahead).start()
    add_row(0)

    @pl.loop(1, side, unroll=3)
    def _(row):
        @pl.when(row + ahead < side)
        def _():
            row_copy(row + ahead).start()

        row_copy(row).wait()
        add_row(row)
        row_out(row - 1).start()

    for at in range(cols):
        done[(side - 1) * cols + at] = sums[side * cols + at].astype(done.dtype)
    row_out(side - 1).start()
    for row in range(side):
        row_out(row).wait()


def grad_conv(turn, messages, source, weights):
    pixels, batch, channels = source.shape
    taps, share, _ = weights[0].shape
    side = math.isqrt(pixels)
    vmem = pl.BlockSpec(memory_space=pltpu.VMEM)
    anywhere = pl.BlockSpec(memory_space=pl.ANY)
    return pl.pallas_call(
        grad_kernel,
        in_specs=[pl.BlockSpec(memory_space=pltpu.SMEM)]
        + [vmem] * 3
        + [anywhere]
        + [vmem] * len(weights),
        out_specs=anywhere,
        out_shape=jax.ShapeDtypeStruct((pixels, share, batch), jnp.bfloat16),
        scratch_shapes=[
            pltpu.VMEM((side, side + 2, batch, channels), jnp.bfloat16),
            pltpu.VMEM((6 * share, 4 * channels), jnp.bfloat16),
            pltpu.VMEM((pixels + 2 * side, share, batch), jnp.float32),
            pltpu.VMEM((pixels, share, batch), jnp.bfloat16),
            pltpu.VMEM((taps, channels, channels), jnp.bfloat16),
            pltpu.SemaphoreType.DMA((side,)),
            pltpu.SemaphoreType.DMA((side,)),
        ],
        compiler_params=pltpu.CompilerParams(vmem_limit_bytes=BIG),
        cost_estimate=pl.CostEstimate(
            flops=2400 * source.size, bytes_accessed=3 * source.size, transcendentals=0
        ),
        name="grad_conv",
    )(turn, *messages, source, *weights)


def conv_kernel(
    own_turn, east, west, across, source, weight, after,
    out, padded, spread, sums, done, sems, out_sems,
):
    rows, cols, batch, channels = padded.shape
    rows -= 2
    cols -= 2
    share = weight.shape[1]
    blocks = rows // 2
    ahead = 2

    def pair_copy(pair):
        row = 2 * pair + 1
        return [
            pltpu.make_async_copy(
                source.at[pl.ds((row + k) * cols, cols)],
                padded.at[row + k + 1, pl.ds(1, cols)],
                sems.at[row + k],
            )
            for k in range(2)
        ]

    def first_copy():
        return pltpu.make_async_copy(
            source.at[pl.ds(0, cols)], padded.at[1, pl.ds(1, cols)], sems.at[0]
        )

    def last_copy():
        return pltpu.make_async_copy(
            source.at[pl.ds((rows - 1) * cols, cols)],
            padded.at[rows, pl.ds(1, cols)],
            sems.at[rows - 1],
        )

    def block_out(block):
        pixels = pl.ds(2 * block * cols, 2 * cols)
        return pltpu.make_async_copy(done.at[pixels], out.at[pixels], out_sems.at[block])

    first_copy().start()
    for pair in range(ahead):
        for copy in pair_copy(pair):
            copy.start()
    tile = jnp.zeros((batch, channels), padded.dtype)
    for row in range(rows + 2):
        padded[row, 0] = tile
        padded[row, cols + 1] = tile
    for col in range(cols):
        padded[0, col + 1] = tile
        padded[rows + 1, col + 1] = tile

    spread[...] = jnp.zeros_like(spread)
    for tap in range(9):
        value = weight[tap]
        for row in range(2):
            for col in range(2):
                to = (row * 2 + col) * share
                at = ((row + tap // 3) * 4 + col + tap % 3) * channels
                spread[to : to + share, at : at + channels] = value
    sums[...] = jnp.zeros_like(sums)
    add_messages(own_turn[0], (east, west, across), sums, 0, share, batch, rows)

    def add_block(block):
        for start in range(0, cols, 4):
            right = jnp.concatenate(
                [
                    jnp.concatenate(
                        [
                            padded[2 * block + row, start + half + col]
                            for row in range(4)
                            for col in range(4)
                        ],
                        axis=1,
                    )
                    for half in (0, 2)
                ],
                axis=0,
            )
            terms = dot(spread[...], right, TURNED)
            for half in (0, 2):
                for row in range(2):
                    for col in range(2):
                        part = terms[
                            (row * 2 + col) * share : (row * 2 + col + 1) * share,
                            half // 2 * batch : (half // 2 + 1) * batch,
                        ]
                        pixel = (2 * block + row) * cols + start + half + col
                        done[pixel] = (sums[pixel] + part).astype(done.dtype)
        block_out(block).start()

    first_copy().wait()

    @pl.loop(0, blocks - 1)
    def _(block):
        @pl.when(block + ahead < blocks - 1)
        def _():
            for copy in pair_copy(block + ahead):
                copy.start()

        @pl.when(block + ahead == blocks - 1)
        def _():
            last_copy().start()

        for copy in pair_copy(block):
            copy.wait()
        add_block(block)

    last_copy().wait()
    add_block(blocks - 1)
    for block in range(blocks):
        block_out(block).wait()


def convolved(turn, messages, source, weight, after):
    pixels, batch, channels = source.shape
    taps, share, _ = weight.shape
    side = math.isqrt(pixels)
    vmem = pl.BlockSpec(memory_space=pltpu.VMEM)
    anywhere = pl.BlockSpec(memory_space=pl.ANY)
    return pl.pallas_call(
        conv_kernel,
        in_specs=[pl.BlockSpec(memory_space=pltpu.SMEM)]
        + [vmem] * 3
        + [anywhere, vmem, anywhere],
        out_specs=anywhere,
        out_shape=jax.ShapeDtypeStruct((pixels, share, batch), jnp.bfloat16),
        scratch_shapes=[
            pltpu.VMEM((side + 2, side + 2, batch, channels), jnp.bfloat16),
            pltpu.VMEM((4 * share, 16 * channels), jnp.bfloat16),
            pltpu.VMEM((pixels, share, batch), jnp.float32),
            pltpu.VMEM((pixels, share, batch), jnp.bfloat16),
            pltpu.SemaphoreType.DMA((side,)),
            pltpu.SemaphoreType.DMA((side // 2,)),
        ],
        compiler_params=pltpu.CompilerParams(vmem_limit_bytes=BIG),
        cost_estimate=pl.CostEstimate(
            flops=2400 * source.size, bytes_accessed=3 * source.size, transcendentals=0
        ),
        name="conv",
    )(turn, *messages, source, weight, after)


def sum_over_tiles(total, count):
    bit = 1
    while bit < count:
        left = count // bit

        def other(flip):
            return lax.ppermute(total, "tile", [(i, i ^ flip) for i in range(count)])

        if left % 4 == 0 and left.bit_length() % 2 == 1:
            near, far, farther = other(bit), other(2 * bit), other(3 * bit)
            total = (total + near) + (far + farther)
            bit *= 4
        else:
            total = total + other(bit)
            bit *= 2
    return total


def per_device(tiles, orientation, weight, grad_out):
    batch, side, _, channels = tiles.shape[1:]
    share = weight.shape[3]
    count = lax.axis_size("tile")
    eastward = [(i, (i + 2) % count) for i in range(count)]
    westward = [(i, (i - 2) % count) for i in range(count)]
    acrossward = [(i, i ^ 1) for i in range(count)]

    def exchanged(sends):
        return [
            lax.ppermute(sends[1], "tile", westward),
            lax.ppermute(sends[0], "tile", eastward),
            lax.ppermute(sends[2], "tile", acrossward),
        ]

    own = weight.transpose(0, 1, 3, 2).reshape(9, share, channels)
    weights = [own] + [
        lax.ppermute(own, "chan", [(i, i ^ flip) for i in range(channels // share)])
        for flip in range(1, channels // share)
    ]
    upstream, turned, *sends = lay_upstream(orientation, weights, grad_out[0])
    grad_messages = exchanged(sends)
    field, edges, inner = lay_field(orientation, tiles[0], turned)
    scale = 1.0 / math.sqrt(count * batch * side * side)
    total, *sends = seam_filters(scale, edges, inner, own, grad_messages)
    conv_messages = exchanged(sends)
    grad = grad_conv(orientation, grad_messages, upstream, weights)
    conv = convolved(orientation, conv_messages, field, own, grad)
    total = sum_over_tiles(total, count)
    shape = (side, side, share, batch)
    conv_out = conv.reshape(shape).transpose(3, 0, 1, 2)[None]
    grad_input = grad.reshape(shape).transpose(3, 0, 1, 2)[None]
    grad_weight = total.reshape(3, 3, share, channels).transpose(0, 1, 3, 2)
    return conv_out, grad_input, grad_weight


def solution(mesh):
    in_specs = (
        P("tile", None, None, None, None),
        P("tile"),
        P(None, None, None, "chan"),
        P("tile", None, None, None, None),
    )
    out_specs = (
        P("tile", None, None, None, "chan"),
        P("tile", None, None, None, "chan"),
        P(None, None, None, "chan"),
    )
    return jax.shard_map(
        per_device, mesh=mesh, in_specs=in_specs, out_specs=out_specs, check_vma=False
    )
```

```python
import math

import jax
import jax.numpy as jnp
from jax import lax
from jax.experimental import pallas as pl
from jax.experimental.pallas import tpu as pltpu
from jax.sharding import PartitionSpec as P

BIG = 56 << 20
AHEAD = 2
EXTRA = 128
FLAT = (((1,), (0,)), ((), ()))
TURNED = (((1,), (1,)), ((), ()))


def dot(left, right, dims):
    return lax.dot_general(left, right, dims, preferred_element_type=jnp.float32)


def stored(turn, row, col, last):

    def chosen(values):
        return jnp.where(
            turn < 2,
            jnp.where(turn == 0, values[0], values[1]),
            jnp.where(turn == 2, values[2], values[3]),
        )

    return (
        chosen((row, last - col, last - row, col)),
        chosen((col, row, last - col, last - row)),
    )


def edge_place(turn, lower, edge, side):
    last = side - 1
    if edge == 0:
        start, after = (0, last), (1, last)
    elif edge == 1:
        start, after = (0, 0), (1, 0)
    else:
        row = last * (1 - lower)
        start, after = (row, 0), (row, 1)
    row, col = stored(turn, *start, last)
    below, beside = stored(turn, *after, last)
    first = row * side + col
    return first, below * side + beside - first


def edge_tap(turn, lower, edge, along, outward):
    if edge == 0:
        cell = (along, 2 if outward else 0)
    elif edge == 1:
        cell = (along, 0 if outward else 2)
    else:
        cell = (2 - 2 * lower if outward else 2 * lower, along)
    row, col = stored(turn, *cell, 2)
    return row * 3 + col


def one_hot(share, channels):
    chan = lax.axis_index("chan").astype(jnp.int32)
    rows = lax.broadcasted_iota(jnp.int32, (share, channels), 0) + chan * share
    cols = lax.broadcasted_iota(jnp.int32, (share, channels), 1)
    return jnp.where(rows == cols, 1.0, 0.0).astype(jnp.bfloat16)


def half_of_band():
    return lax.axis_index("tile").astype(jnp.int32) % 2


def later(value, width):
    empty = jnp.zeros((value.shape[0], width), value.dtype)
    return jnp.concatenate([empty, value[:, :-width]], axis=1)


def earlier(value, width):
    empty = jnp.zeros((value.shape[0], width), value.dtype)
    return jnp.concatenate([value[:, width:], empty], axis=1)


def terms_of(product, share, batch):
    return (
        later(product[:share], batch)
        + product[share : 2 * share]
        + earlier(product[2 * share : 3 * share], batch)
    ).astype(jnp.bfloat16)


def gather_filters(parts, whole):
    taps, share, _ = parts[0].shape
    chan = lax.axis_index("chan").astype(jnp.int32)
    for flip, part in enumerate(parts):
        start = pl.multiple_of((chan ^ flip) * share, share)
        for tap in range(taps):
            whole[tap, pl.ds(start, share)] = part[tap]


def pair_in(source, stage, sems, pair):
    return pltpu.make_async_copy(
        source.at[:, pl.ds(2 * pair, 2)], stage.at[pair], sems.at[pair]
    )


def edge_columns(turn, lower, edge, flat, side, batch):
    first, step = edge_place(turn, lower, edge, side)
    parts = []
    for pos in range(side):
        pixel = first + pos * step
        col = pl.multiple_of(lax.rem(pixel, side) * batch, batch)
        parts.append(flat[lax.div(pixel, side), :, pl.ds(col, batch)])
    return jnp.concatenate(parts, axis=1)


def turned_out(flat, turned, sems, pair):
    part = pl.ds(2 * pair, 2)
    return pltpu.make_async_copy(flat.at[part], turned.at[part], sems.at[pair])


def upstream_kernel(
    own_turn, weight, other1, other2, other3, upstream,
    turned, east, west, across,
    stage, held, flat, whole, rowed, shuffle, same, in_sems, turned_sems,
):
    pairs, batch, rows, side, channels = stage.shape
    taps, share, _ = weight.shape
    group = 256 // side
    for pair in range(AHEAD):
        pair_in(upstream, stage, in_sems, pair).start()
    to = lax.broadcasted_iota(jnp.int32, (256, 256), 0)
    come = lax.broadcasted_iota(jnp.int32, (256, 256), 1)
    moves = (to // group == come % side) & (to % group == come // side)
    shuffle[...] = jnp.where(moves, 1.0, 0.0).astype(jnp.bfloat16)
    to = lax.broadcasted_iota(jnp.int32, (channels, channels), 0)
    come = lax.broadcasted_iota(jnp.int32, (channels, channels), 1)
    same[...] = jnp.where(to == come, 1.0, 0.0).astype(jnp.bfloat16)
    pick = one_hot(share, channels)
    gather_filters((weight, other1, other2, other3), whole)
    for tap in range(taps):
        rowed[tap] = dot(pick, whole[tap], TURNED).astype(jnp.bfloat16)

    @pl.loop(0, pairs)
    def _(pair):
        @pl.when(pair + AHEAD < pairs)
        def _():
            pair_in(upstream, stage, in_sems, pair + AHEAD).start()

        pair_in(upstream, stage, in_sems, pair).wait()
        for start in range(0, batch, group):
            block = jnp.concatenate(
                [
                    stage[pair, start : start + group, row].reshape(256, channels)
                    for row in range(rows)
                ],
                axis=1,
            )
            moved = dot(shuffle[...], block, FLAT).astype(jnp.bfloat16)
            for row in range(rows):
                held[row * side : (row + 1) * side, start : start + group] = moved[
                    :, row * channels : (row + 1) * channels
                ].reshape(side, group, channels)
        for row in range(rows):
            flat[2 * pair + row] = dot(
                same[...],
                held[row * side : (row + 1) * side].reshape(side * batch, channels),
                TURNED,
            ).astype(jnp.bfloat16)
        turned_out(flat, turned, turned_sems, pair).start()

    lower = half_of_band()
    turn = own_turn[0]
    for edge, out in enumerate((east, west, across)):
        filters = jnp.concatenate(
            [rowed[edge_tap(turn, lower, edge, 2 - d, True)] for d in range(3)] + [pick],
            axis=0,
        )
        product = dot(filters, edge_columns(turn, lower, edge, flat, side, batch), FLAT)
        out[0:share, 0 : side * batch] = terms_of(product, share, batch)
        out[share:, 0 : side * batch] = product[3 * share :].astype(jnp.bfloat16)
        code = jnp.full((2 * share, EXTRA), turn, jnp.int32)
        out[:, side * batch :] = code.astype(jnp.float32).astype(jnp.bfloat16)
    for pair in range(pairs):
        turned_out(flat, turned, turned_sems, pair).wait()


def lay_upstream(turn, weights, upstream):
    batch, side, _, channels = upstream.shape
    taps, share, _ = weights[0].shape
    smem = pl.BlockSpec(memory_space=pltpu.SMEM)
    vmem = pl.BlockSpec(memory_space=pltpu.VMEM)
    anywhere = pl.BlockSpec(memory_space=pl.ANY)
    pairs = side // 2
    turned = jax.ShapeDtypeStruct((side, channels, side * batch), jnp.bfloat16)
    message = jax.ShapeDtypeStruct((2 * share, side * batch + EXTRA), jnp.bfloat16)
    return pl.pallas_call(
        upstream_kernel,
        in_specs=[smem] + [vmem] * len(weights) + [anywhere],
        out_specs=[anywhere] + [vmem] * 3,
        out_shape=[turned] + [message] * 3,
        scratch_shapes=[
            pltpu.VMEM((pairs, batch, 2, side, channels), jnp.bfloat16),
            pltpu.VMEM((2 * side, batch, channels), jnp.bfloat16),
            pltpu.VMEM(turned.shape, jnp.bfloat16),
            pltpu.VMEM((taps, channels, channels), jnp.bfloat16),
            pltpu.VMEM((taps, share, channels), jnp.bfloat16),
            pltpu.VMEM((256, 256), jnp.bfloat16),
            pltpu.VMEM((channels, channels), jnp.bfloat16),
            pltpu.SemaphoreType.DMA((pairs,)),
            pltpu.SemaphoreType.DMA((pairs,)),
        ],
        compiler_params=pltpu.CompilerParams(vmem_limit_bytes=BIG),
        cost_estimate=pl.CostEstimate(
            flops=1024 * upstream.size, bytes_accessed=4 * upstream.size, transcendentals=0
        ),
        name="lay_upstream",
    )(turn, *weights, upstream)


def field_kernel(
    own_turn, field, turned, laid, edges, inner,
    stage, held, flat, padded, total, in_sems, out_sems, turned_sem, edge_sems,
):
    pairs, batch, rows, side, channels = stage.shape
    share = padded.shape[1]
    width = side * batch
    chan = lax.axis_index("chan").astype(jnp.int32)
    own = pl.ds(pl.multiple_of(chan * share, share), share)
    turned_in = pltpu.make_async_copy(
        turned.at[:, own], padded.at[pl.ds(1, side), :, pl.ds(batch, width)], turned_sem
    )
    pair_in(field, stage, in_sems, 0).start()
    turned_in.start()
    for pair in range(1, AHEAD):
        pair_in(field, stage, in_sems, pair).start()
    padded[0] = jnp.zeros(padded.shape[1:], padded.dtype)
    padded[side + 1] = jnp.zeros(padded.shape[1:], padded.dtype)
    column = jnp.zeros((side, share, batch), padded.dtype)
    padded[1 : side + 1, :, 0:batch] = column
    padded[1 : side + 1, :, width + batch :] = column
    total[...] = jnp.zeros_like(total)

    def lay(pair):
        pair_in(field, stage, in_sems, pair).wait()
        for row in range(rows):
            block = jnp.swapaxes(stage[pair, :, row], 0, 1)
            held[pl.ds((2 * pair + row) * side, side)] = block
            for col in range(side):
                flat[2 * pair + row, :, col * batch : (col + 1) * batch] = block[col].T
        turned_out(flat, laid, out_sems, pair).start()

    def add_filters(pair):
        cols = 8
        for start in range(0, side, cols):
            right = jnp.concatenate(
                [
                    held[pl.ds((2 * pair + row) * side + start, cols)].reshape(
                        cols * batch, channels
                    )
                    for row in range(rows)
                ],
                axis=1,
            )
            parts = []
            for tap in range(3):
                at = (start + 2 - tap) * batch
                for half in range(2):
                    part = padded[pl.ds(2 * pair + 2 * half, 2), :, at : at + cols * batch]
                    parts.append(part.reshape(2 * share, cols * batch))
            for half in range(2):
                left = jnp.concatenate(parts[3 * half : 3 * half + 3], axis=0)
                total[6 * share * half : 6 * share * (half + 1)] += dot(left, right, FLAT)

    lay(0)
    turned_in.wait()

    @pl.loop(1, pairs)
    def _(pair):
        @pl.when(pair + AHEAD - 1 < pairs)
        def _():
            pair_in(field, stage, in_sems, pair + AHEAD - 1).start()

        add_filters(pair - 1)
        lay(pair)

    lower = half_of_band()
    turn = own_turn[0]
    for edge in range(3):
        first, step = edge_place(turn, lower, edge, side)
        for pos in range(side):
            pltpu.make_async_copy(
                held.at[first + pos * step], edges.at[edge, pos], edge_sems.at[edge]
            ).start()
    add_filters(pairs - 1)
    for row_tap in range(3):
        for col_tap in range(3):
            value = jnp.zeros((share, channels), jnp.float32)
            for row in range(rows):
                start = col_tap * (rows + 2) * share + (row + 2 - row_tap) * share
                value += total[start : start + share, row * channels : (row + 1) * channels]
            inner[row_tap * 3 + col_tap] = value
    for pair in range(pairs):
        turned_out(flat, laid, out_sems, pair).wait()
    for edge in range(3):
        pltpu.make_async_copy(
            held.at[pl.ds(0, side)], edges.at[edge], edge_sems.at[edge]
        ).wait()


def lay_field(turn, field, turned, share):
    batch, side, _, channels = field.shape
    anywhere = pl.BlockSpec(memory_space=pl.ANY)
    pairs = side // 2
    laid = jax.ShapeDtypeStruct((side, channels, side * batch), jnp.bfloat16)
    edges = jax.ShapeDtypeStruct((3, side, batch, channels), jnp.bfloat16)
    inner = jax.ShapeDtypeStruct((9, share, channels), jnp.float32)
    return pl.pallas_call(
        field_kernel,
        in_specs=[pl.BlockSpec(memory_space=pltpu.SMEM)] + [anywhere] * 2,
        out_specs=[anywhere] * 2 + [pl.BlockSpec(memory_space=pltpu.VMEM)],
        out_shape=[laid, edges, inner],
        scratch_shapes=[
            pltpu.VMEM((pairs, batch, 2, side, channels), jnp.bfloat16),
            pltpu.VMEM((side * side, batch, channels), jnp.bfloat16),
            pltpu.VMEM(laid.shape, jnp.bfloat16),
            pltpu.VMEM((side + 2, share, (side + 2) * batch), jnp.bfloat16),
            pltpu.VMEM((12 * share, 2 * channels), jnp.float32),
            pltpu.SemaphoreType.DMA((pairs,)),
            pltpu.SemaphoreType.DMA((pairs,)),
            pltpu.SemaphoreType.DMA,
            pltpu.SemaphoreType.DMA((3,)),
        ],
        compiler_params=pltpu.CompilerParams(vmem_limit_bytes=BIG),
        cost_estimate=pl.CostEstimate(
            flops=1800 * field.size, bytes_accessed=5 * field.size, transcendentals=0
        ),
        name="lay_field",
    )(turn, field, turned)


def seam_kernel(scale, edges, inner, weight, *refs):
    messages, out, terms_out = refs[:3], refs[3], refs[4:7]
    side, batch, channels = edges.shape[1:]
    share = out.shape[1]
    width = side * batch
    lower = half_of_band()
    out[...] = inner[...]
    for edge, message in enumerate(messages):
        turn = jnp.max(message[0:16, width:].astype(jnp.float32)).astype(jnp.int32)
        taps = [edge_tap(turn, lower, edge, d, False) for d in range(3)]
        turned = message[share:, 0:width]
        left = jnp.concatenate([earlier(turned, batch), turned, later(turned, batch)], axis=0)
        pixels = edges[edge].reshape(width, channels)
        terms = dot(left, pixels, FLAT)
        for d in range(3):
            out[taps[d]] += terms[d * share : (d + 1) * share]
        filters = jnp.concatenate([weight[tap] for tap in taps], axis=0)
        terms_out[edge][...] = terms_of(dot(filters, pixels, TURNED), share, batch)
    out[...] = out[...] * scale


def seam_filters(scale, edges, inner, weight, messages):
    _, side, batch, channels = edges.shape
    share = inner.shape[1]
    vmem = pl.BlockSpec(memory_space=pltpu.VMEM)

    def body(*refs):
        seam_kernel(scale, *refs)

    return pl.pallas_call(
        body,
        in_specs=[vmem] * 6,
        out_specs=[vmem] * 4,
        out_shape=[jax.ShapeDtypeStruct(inner.shape, jnp.float32)]
        + [jax.ShapeDtypeStruct((share, side * batch), jnp.bfloat16)] * 3,
        compiler_params=pltpu.CompilerParams(vmem_limit_bytes=BIG),
        cost_estimate=pl.CostEstimate(
            flops=36 * share * side * batch * channels,
            bytes_accessed=6 * side * batch * channels,
            transcendentals=0,
        ),
        name="seam_filters",
    )(edges, inner, weight, *messages)


def add_messages(turn, messages, sums, offset, share, batch, side):
    lower = half_of_band()
    for edge, message in enumerate(messages):
        first, step = edge_place(turn, lower, edge, side)
        for pos in range(side):
            sums[first + pos * step + offset] += message[
                0:share, pos * batch : (pos + 1) * batch
            ].astype(jnp.float32)


def conv_kernel(mirrored, own_turn, east, west, across, source, *refs):
    out, padded, spread, sums, done, whole, sems, out_sems = refs[-8:]
    weights = refs[:-8]
    side, channels, lanes = padded.shape
    share, batch = done.shape[1:]
    cols = lanes // batch - 2
    ahead = 3

    def row_copy(row):
        return pltpu.make_async_copy(
            source.at[row], padded.at[row, :, pl.ds(batch, cols * batch)], sems.at[row]
        )

    def row_out(row):
        pixels = pl.ds(row * cols, cols)
        return pltpu.make_async_copy(done.at[pixels], out.at[pixels], out_sems.at[row])

    for row in range(ahead):
        row_copy(row).start()
    tile = jnp.zeros((channels, batch), padded.dtype)
    for row in range(side):
        padded[row, :, 0:batch] = tile
        padded[row, :, lanes - batch :] = tile

    if mirrored:
        gather_filters(weights, whole)
        pick = one_hot(share, channels)
        blocks = [dot(pick, whole[8 - tap], TURNED).astype(jnp.bfloat16) for tap in range(9)]
    else:
        blocks = [weights[0][tap] for tap in range(9)]
    empty = jnp.zeros((share, channels), spread.dtype)
    for row in range(3):
        for out_col in range(2):
            for in_col in range(4):
                tap = in_col - out_col
                to = (row * 2 + out_col) * share
                at = in_col * channels
                spread[to : to + share, at : at + channels] = (
                    blocks[row * 3 + tap] if 0 <= tap <= 2 else empty
                )
    sums[...] = jnp.zeros_like(sums)
    add_messages(own_turn[0], (east, west, across), sums, cols, share, batch, side)

    def add_row(row):
        for start in range(0, cols, 4):
            right = jnp.concatenate(
                [
                    jnp.concatenate(
                        [
                            padded[
                                row,
                                :,
                                (start + half + col) * batch : (start + half + col + 1) * batch,
                            ]
                            for half in (0, 2)
                        ],
                        axis=1,
                    )
                    for col in range(4)
                ],
                axis=0,
            )
            terms = dot(spread[...], right, FLAT)
            for half in (0, 2):
                for col in range(2):
                    part = [
                        terms[
                            (k * 2 + col) * share : (k * 2 + col + 1) * share,
                            half // 2 * batch : (half // 2 + 1) * batch,
                        ]
                        for k in range(3)
                    ]
                    at = start + half + col
                    pixel = row * cols + at
                    sums[pixel + 2 * cols] += part[0]
                    sums[pixel + cols] += part[1]
                    done[jnp.maximum(pixel - cols, at)] = (sums[pixel] + part[2]).astype(
                        done.dtype
                    )

    row_copy(0).wait()
    row_copy(ahead).start()
    add_row(0)

    @pl.loop(1, side, unroll=3)
    def _(row):
        @pl.when(row + ahead < side)
        def _():
            row_copy(row + ahead).start()

        row_copy(row).wait()
        add_row(row)
        row_out(row - 1).start()

    for at in range(cols):
        done[(side - 1) * cols + at] = sums[side * cols + at].astype(done.dtype)
    row_out(side - 1).start()
    for row in range(side):
        row_out(row).wait()


def convolved(mirrored, turn, messages, source, weights, *after):
    side, channels, width = source.shape
    taps, share, _ = weights[0].shape
    batch = width // side
    pixels = side * side
    vmem = pl.BlockSpec(memory_space=pltpu.VMEM)
    anywhere = pl.BlockSpec(memory_space=pl.ANY)

    def body(*refs):
        conv_kernel(mirrored, *refs)

    return pl.pallas_call(
        body,
        in_specs=[pl.BlockSpec(memory_space=pltpu.SMEM)]
        + [vmem] * 3
        + [anywhere]
        + [vmem] * len(weights)
        + [anywhere] * len(after),
        out_specs=anywhere,
        out_shape=jax.ShapeDtypeStruct((pixels, share, batch), jnp.bfloat16),
        scratch_shapes=[
            pltpu.VMEM((side, channels, width + 2 * batch), jnp.bfloat16),
            pltpu.VMEM((6 * share, 4 * channels), jnp.bfloat16),
            pltpu.VMEM((pixels + 2 * side, share, batch), jnp.float32),
            pltpu.VMEM((pixels, share, batch), jnp.bfloat16),
            pltpu.VMEM((taps, channels, channels), jnp.bfloat16),
            pltpu.SemaphoreType.DMA((side,)),
            pltpu.SemaphoreType.DMA((side,)),
        ],
        compiler_params=pltpu.CompilerParams(vmem_limit_bytes=BIG),
        cost_estimate=pl.CostEstimate(
            flops=2400 * source.size, bytes_accessed=3 * source.size, transcendentals=0
        ),
        name="grad_conv" if mirrored else "conv",
    )(turn, *messages, source, *weights, *after)


def sum_over_tiles(total, count):
    bit = 1
    while bit < count:
        left = count // bit

        def other(flip):
            return lax.ppermute(total, "tile", [(i, i ^ flip) for i in range(count)])

        if left % 4 == 0 and left.bit_length() % 2 == 1:
            near, far, farther = other(bit), other(2 * bit), other(3 * bit)
            total = (total + near) + (far + farther)
            bit *= 4
        else:
            total = total + other(bit)
            bit *= 2
    return total


def per_device(tiles, orientation, weight, grad_out):
    batch, side, _, channels = tiles.shape[1:]
    share = weight.shape[3]
    count = lax.axis_size("tile")
    eastward = [(i, (i + 2) % count) for i in range(count)]
    westward = [(i, (i - 2) % count) for i in range(count)]
    acrossward = [(i, i ^ 1) for i in range(count)]

    def exchanged(sends):
        return [
            lax.ppermute(sends[1], "tile", westward),
            lax.ppermute(sends[0], "tile", eastward),
            lax.ppermute(sends[2], "tile", acrossward),
        ]

    own = weight.transpose(0, 1, 3, 2).reshape(9, share, channels)
    weights = [own] + [
        lax.ppermute(own, "chan", [(i, i ^ flip) for i in range(channels // share)])
        for flip in range(1, channels // share)
    ]
    upstream, *sends = lay_upstream(orientation, weights, grad_out[0])
    grad_messages = exchanged(sends)
    field, edges, inner = lay_field(orientation, tiles[0], upstream, share)
    scale = 1.0 / math.sqrt(count * batch * side * side)
    total, *sends = seam_filters(scale, edges, inner, own, grad_messages)
    conv_messages = exchanged(sends)
    grad = convolved(True, orientation, grad_messages, upstream, weights)
    conv = convolved(False, orientation, conv_messages, field, weights[:1], grad)
    total = sum_over_tiles(total, count)
    shape = (side, side, share, batch)
    conv_out = conv.reshape(shape).transpose(3, 0, 1, 2)[None]
    grad_input = grad.reshape(shape).transpose(3, 0, 1, 2)[None]
    grad_weight = total.reshape(3, 3, share, channels).transpose(0, 1, 3, 2)
    return conv_out, grad_input, grad_weight


def solution(mesh):
    in_specs = (
        P("tile", None, None, None, None),
        P("tile"),
        P(None, None, None, "chan"),
        P("tile", None, None, None, None),
    )
    out_specs = (
        P("tile", None, None, None, "chan"),
        P("tile", None, None, None, "chan"),
        P(None, None, None, "chan"),
    )
    return jax.shard_map(
        per_device, mesh=mesh, in_specs=in_specs, out_specs=out_specs, check_vma=False
    )
```

```python
import math

import jax
import jax.numpy as jnp
from jax import lax
from jax.experimental import pallas as pl
from jax.experimental.pallas import tpu as pltpu
from jax.sharding import PartitionSpec as P

BIG = 56 << 20
AHEAD = 2
EXTRA = 128
FLAT = (((1,), (0,)), ((), ()))
TURNED = (((1,), (1,)), ((), ()))


def dot(left, right, dims):
    return lax.dot_general(left, right, dims, preferred_element_type=jnp.float32)


def stored(turn, row, col, last):

    def chosen(values):
        return jnp.where(
            turn < 2,
            jnp.where(turn == 0, values[0], values[1]),
            jnp.where(turn == 2, values[2], values[3]),
        )

    return (
        chosen((row, last - col, last - row, col)),
        chosen((col, row, last - col, last - row)),
    )


def edge_place(turn, lower, edge, side):
    last = side - 1
    if edge == 0:
        start, after = (0, last), (1, last)
    elif edge == 1:
        start, after = (0, 0), (1, 0)
    else:
        row = last * (1 - lower)
        start, after = (row, 0), (row, 1)
    row, col = stored(turn, *start, last)
    below, beside = stored(turn, *after, last)
    first = row * side + col
    return first, below * side + beside - first


def edge_tap(turn, lower, edge, along, outward):
    if edge == 0:
        cell = (along, 2 if outward else 0)
    elif edge == 1:
        cell = (along, 0 if outward else 2)
    else:
        cell = (2 - 2 * lower if outward else 2 * lower, along)
    row, col = stored(turn, *cell, 2)
    return row * 3 + col


def one_hot(share, channels):
    chan = lax.axis_index("chan").astype(jnp.int32)
    rows = lax.broadcasted_iota(jnp.int32, (share, channels), 0) + chan * share
    cols = lax.broadcasted_iota(jnp.int32, (share, channels), 1)
    return jnp.where(rows == cols, 1.0, 0.0).astype(jnp.bfloat16)


def half_of_band():
    return lax.axis_index("tile").astype(jnp.int32) % 2


def later(value, width):
    empty = jnp.zeros((value.shape[0], width), value.dtype)
    return jnp.concatenate([empty, value[:, :-width]], axis=1)


def earlier(value, width):
    empty = jnp.zeros((value.shape[0], width), value.dtype)
    return jnp.concatenate([value[:, width:], empty], axis=1)


def terms_of(product, share, batch):
    return (
        later(product[:share], batch)
        + product[share : 2 * share]
        + earlier(product[2 * share : 3 * share], batch)
    ).astype(jnp.bfloat16)


def gather_filters(parts, whole):
    taps, share, _ = parts[0].shape
    chan = lax.axis_index("chan").astype(jnp.int32)
    for flip, part in enumerate(parts):
        start = pl.multiple_of((chan ^ flip) * share, share)
        for tap in range(taps):
            whole[tap, pl.ds(start, share)] = part[tap]


def pair_in(source, stage, sems, pair):
    return pltpu.make_async_copy(
        source.at[:, pl.ds(2 * pair, 2)], stage.at[pair], sems.at[pair]
    )


def turned_out(flat, turned, sems, pair):
    part = pl.ds(2 * pair, 2)
    return pltpu.make_async_copy(flat.at[part], turned.at[part], sems.at[pair])


def lay_pair(stage, held, flat, pair):
    _, batch, rows, side, _ = stage.shape
    for row in range(rows):
        block = jnp.swapaxes(stage[pair, :, row], 0, 1)
        if held is not None:
            held[pl.ds((2 * pair + row) * side, side)] = block
        for col in range(side):
            flat[2 * pair + row, :, col * batch : (col + 1) * batch] = block[col].T


def upstream_kernel(
    own_turn, upstream, turned, edges, east, west, across,
    stage, flat, in_sems, turned_sems, edge_sems,
):
    pairs, batch, rows, side, channels = stage.shape
    share = east.shape[0]
    for pair in range(AHEAD):
        pair_in(upstream, stage, in_sems, pair).start()

    @pl.loop(0, pairs)
    def _(pair):
        @pl.when(pair + AHEAD < pairs)
        def _():
            pair_in(upstream, stage, in_sems, pair + AHEAD).start()

        pair_in(upstream, stage, in_sems, pair).wait()
        lay_pair(stage, None, flat, pair)
        turned_out(flat, turned, turned_sems, pair).start()

    chan = lax.axis_index("chan").astype(jnp.int32)
    own = pl.ds(pl.multiple_of(chan * share, share), share)
    lower = half_of_band()
    turn = own_turn[0]
    for edge, out in enumerate((east, west, across)):
        first, step = edge_place(turn, lower, edge, side)
        for pos in range(side):
            pixel = first + pos * step
            row = lax.div(pixel, side)
            col = pl.ds(pl.multiple_of(lax.rem(pixel, side) * batch, batch), batch)
            lanes = pl.ds(pos * batch, batch)
            pltpu.make_async_copy(
                flat.at[row, :, col], edges.at[edge, :, lanes], edge_sems.at[edge]
            ).start()
            out[:, lanes] = flat[row, own, col]
        code = jnp.full((share, EXTRA), turn, jnp.int32)
        out[:, side * batch :] = code.astype(jnp.float32).astype(jnp.bfloat16)
    for pair in range(pairs):
        turned_out(flat, turned, turned_sems, pair).wait()
    for edge in range(3):
        pltpu.make_async_copy(flat.at[0], edges.at[edge], edge_sems.at[edge]).wait()


def lay_upstream(turn, upstream, share):
    batch, side, _, channels = upstream.shape
    vmem = pl.BlockSpec(memory_space=pltpu.VMEM)
    anywhere = pl.BlockSpec(memory_space=pl.ANY)
    pairs = side // 2
    turned = jax.ShapeDtypeStruct((side, channels, side * batch), jnp.bfloat16)
    edges = jax.ShapeDtypeStruct((3, channels, side * batch), jnp.bfloat16)
    message = jax.ShapeDtypeStruct((share, side * batch + EXTRA), jnp.bfloat16)
    return pl.pallas_call(
        upstream_kernel,
        in_specs=[pl.BlockSpec(memory_space=pltpu.SMEM), anywhere],
        out_specs=[anywhere] * 2 + [vmem] * 3,
        out_shape=[turned, edges] + [message] * 3,
        scratch_shapes=[
            pltpu.VMEM((pairs, batch, 2, side, channels), jnp.bfloat16),
            pltpu.VMEM(turned.shape, jnp.bfloat16),
            pltpu.SemaphoreType.DMA((pairs,)),
            pltpu.SemaphoreType.DMA((pairs,)),
            pltpu.SemaphoreType.DMA((3,)),
        ],
        compiler_params=pltpu.CompilerParams(vmem_limit_bytes=BIG),
        cost_estimate=pl.CostEstimate(
            flops=1024 * upstream.size, bytes_accessed=4 * upstream.size, transcendentals=0
        ),
        name="lay_upstream",
    )(turn, upstream)


def field_kernel(
    own_turn, weight, other1, other2, other3, field, turned, laid, edges, inner, rowed,
    stage, held, flat, padded, total, whole, in_sems, out_sems, turned_sem, edge_sems,
):
    pairs, batch, rows, side, channels = stage.shape
    share = padded.shape[1]
    width = side * batch
    chan = lax.axis_index("chan").astype(jnp.int32)
    own = pl.ds(pl.multiple_of(chan * share, share), share)
    turned_in = pltpu.make_async_copy(
        turned.at[:, own], padded.at[pl.ds(1, side), :, pl.ds(batch, width)], turned_sem
    )
    pair_in(field, stage, in_sems, 0).start()
    turned_in.start()
    for pair in range(1, AHEAD):
        pair_in(field, stage, in_sems, pair).start()
    padded[0] = jnp.zeros(padded.shape[1:], padded.dtype)
    padded[side + 1] = jnp.zeros(padded.shape[1:], padded.dtype)
    column = jnp.zeros((side, share, batch), padded.dtype)
    padded[1 : side + 1, :, 0:batch] = column
    padded[1 : side + 1, :, width + batch :] = column
    total[...] = jnp.zeros_like(total)

    def lay(pair):
        pair_in(field, stage, in_sems, pair).wait()
        lay_pair(stage, held, flat, pair)
        turned_out(flat, laid, out_sems, pair).start()

    def add_filters(pair):
        cols = 8
        for start in range(0, side, cols):
            right = jnp.concatenate(
                [
                    held[pl.ds((2 * pair + row) * side + start, cols)].reshape(
                        cols * batch, channels
                    )
                    for row in range(rows)
                ],
                axis=1,
            )
            parts = []
            for tap in range(3):
                at = (start + 2 - tap) * batch
                for half in range(2):
                    part = padded[pl.ds(2 * pair + 2 * half, 2), :, at : at + cols * batch]
                    parts.append(part.reshape(2 * share, cols * batch))
            for half in range(2):
                left = jnp.concatenate(parts[3 * half : 3 * half + 3], axis=0)
                total[6 * share * half : 6 * share * (half + 1)] += dot(left, right, FLAT)

    gather_filters((weight, other1, other2, other3), whole)
    pick = one_hot(share, channels)
    for tap in range(9):
        rowed[tap] = dot(pick, whole[tap], TURNED).astype(jnp.bfloat16)
    lay(0)
    turned_in.wait()

    @pl.loop(1, pairs)
    def _(pair):
        @pl.when(pair + AHEAD - 1 < pairs)
        def _():
            pair_in(field, stage, in_sems, pair + AHEAD - 1).start()

        add_filters(pair - 1)
        lay(pair)

    lower = half_of_band()
    turn = own_turn[0]
    for edge in range(3):
        first, step = edge_place(turn, lower, edge, side)
        for pos in range(side):
            pltpu.make_async_copy(
                held.at[first + pos * step], edges.at[edge, pos], edge_sems.at[edge]
            ).start()
    add_filters(pairs - 1)
    for row_tap in range(3):
        for col_tap in range(3):
            value = jnp.zeros((share, channels), jnp.float32)
            for row in range(rows):
                start = col_tap * (rows + 2) * share + (row + 2 - row_tap) * share
                value += total[start : start + share, row * channels : (row + 1) * channels]
            inner[row_tap * 3 + col_tap] = value
    for pair in range(pairs):
        turned_out(flat, laid, out_sems, pair).wait()
    for edge in range(3):
        pltpu.make_async_copy(
            held.at[pl.ds(0, side)], edges.at[edge], edge_sems.at[edge]
        ).wait()


def lay_field(turn, weights, field, turned):
    share = weights[0].shape[1]
    vmem = pl.BlockSpec(memory_space=pltpu.VMEM)
    batch, side, _, channels = field.shape
    anywhere = pl.BlockSpec(memory_space=pl.ANY)
    pairs = side // 2
    laid = jax.ShapeDtypeStruct((side, channels, side * batch), jnp.bfloat16)
    edges = jax.ShapeDtypeStruct((3, side, batch, channels), jnp.bfloat16)
    inner = jax.ShapeDtypeStruct((9, share, channels), jnp.float32)
    return pl.pallas_call(
        field_kernel,
        in_specs=[pl.BlockSpec(memory_space=pltpu.SMEM)]
        + [vmem] * len(weights)
        + [anywhere] * 2,
        out_specs=[anywhere] * 2 + [vmem] * 2,
        out_shape=[laid, edges, inner, jax.ShapeDtypeStruct(inner.shape, jnp.bfloat16)],
        scratch_shapes=[
            pltpu.VMEM((pairs, batch, 2, side, channels), jnp.bfloat16),
            pltpu.VMEM((side * side, batch, channels), jnp.bfloat16),
            pltpu.VMEM(laid.shape, jnp.bfloat16),
            pltpu.VMEM((side + 2, share, (side + 2) * batch), jnp.bfloat16),
            pltpu.VMEM((12 * share, 2 * channels), jnp.float32),
            pltpu.VMEM((9, channels, channels), jnp.bfloat16),
            pltpu.SemaphoreType.DMA((pairs,)),
            pltpu.SemaphoreType.DMA((pairs,)),
            pltpu.SemaphoreType.DMA,
            pltpu.SemaphoreType.DMA((3,)),
        ],
        compiler_params=pltpu.CompilerParams(vmem_limit_bytes=BIG),
        cost_estimate=pl.CostEstimate(
            flops=1800 * field.size, bytes_accessed=5 * field.size, transcendentals=0
        ),
        name="lay_field",
    )(turn, *weights, field, turned)


def seam_kernel(scale, own_turn, edges, upstream_edges, inner, weight, rowed, *refs):
    messages, out, terms_out = refs[:3], refs[3], refs[4:7]
    side, batch, channels = edges.shape[1:]
    share = out.shape[1]
    width = side * batch
    lower = half_of_band()
    out[...] = inner[...]
    for edge, message in enumerate(messages):
        turn = jnp.max(message[0:16, width:].astype(jnp.float32)).astype(jnp.int32)
        taps = [edge_tap(turn, lower, edge, d, False) for d in range(3)]
        turned = message[:, 0:width]
        left = jnp.concatenate([earlier(turned, batch), turned, later(turned, batch)], axis=0)
        pixels = edges[edge].reshape(width, channels)
        terms = dot(left, pixels, FLAT)
        for d in range(3):
            out[taps[d]] += terms[d * share : (d + 1) * share]
        filters = jnp.concatenate([weight[tap] for tap in taps], axis=0)
        terms_out[edge][0:share] = terms_of(dot(filters, pixels, TURNED), share, batch)
        filters = jnp.concatenate(
            [rowed[edge_tap(own_turn[0], lower, edge, 2 - d, True)] for d in range(3)], axis=0
        )
        terms_out[edge][share:] = terms_of(
            dot(filters, upstream_edges[edge], FLAT), share, batch
        )
    out[...] = out[...] * scale


def seam_filters(scale, turn, edges, upstream_edges, inner, weight, rowed, messages):
    _, side, batch, channels = edges.shape
    share = inner.shape[1]
    vmem = pl.BlockSpec(memory_space=pltpu.VMEM)

    def body(*refs):
        seam_kernel(scale, *refs)

    return pl.pallas_call(
        body,
        in_specs=[pl.BlockSpec(memory_space=pltpu.SMEM)] + [vmem] * 8,
        out_specs=[vmem] * 4,
        out_shape=[jax.ShapeDtypeStruct(inner.shape, jnp.float32)]
        + [jax.ShapeDtypeStruct((2 * share, side * batch), jnp.bfloat16)] * 3,
        compiler_params=pltpu.CompilerParams(vmem_limit_bytes=BIG),
        cost_estimate=pl.CostEstimate(
            flops=54 * share * side * batch * channels,
            bytes_accessed=12 * side * batch * channels,
            transcendentals=0,
        ),
        name="seam_filters",
    )(turn, edges, upstream_edges, inner, weight, rowed, *messages)


def border_rows(cols, rows, source, target, sems):
    copies = []
    for index, row in enumerate((0, rows - 1)):
        where = pl.ds(row * cols, cols)
        copies.append(
            pltpu.make_async_copy(source.at[where], target.at[where], sems.at[index])
        )
    return copies


def start_border(cols, rows, source, target, sems):
    for copy in border_rows(cols, rows, source, target, sems):
        copy.start()
    for row in range(1, rows - 1):
        for col in (0, cols - 1):
            where = pl.ds(row * cols + col, 1)
            pltpu.make_async_copy(source.at[where], target.at[where], sems.at[2]).start()


def wait_border(cols, rows, source, target, sems):
    for copy in border_rows(cols, rows, source, target, sems):
        copy.wait()
    between = pl.ds(cols, 2 * (rows - 2))
    pltpu.make_async_copy(source.at[between], target.at[between], sems.at[2]).wait()


def conv_kernel(last, *refs):
    if last:
        own_turn, east, west, across, source, weight, other_in = refs[:7]
        out, other_out, padded, spread, sums, done, sems, out_sems = refs[7:15]
        other, other_sems, back_sems = refs[15:]
    else:
        source, weight, out, padded, spread, sums, done, sems, out_sems = refs
    side, channels, lanes = padded.shape
    share, batch = done.shape[1:]
    cols = lanes // batch - 2
    ahead = 3

    def row_copy(row):
        return pltpu.make_async_copy(
            source.at[row], padded.at[row, :, pl.ds(batch, cols * batch)], sems.at[row]
        )

    def row_out(row):
        pixels = pl.ds(row * cols, cols)
        return pltpu.make_async_copy(done.at[pixels], out.at[pixels], out_sems.at[row])

    for row in range(ahead):
        row_copy(row).start()
    tile = jnp.zeros((channels, batch), padded.dtype)
    for row in range(side):
        padded[row, :, 0:batch] = tile
        padded[row, :, lanes - batch :] = tile

    blocks = [weight[tap if last else 8 - tap] for tap in range(9)]
    empty = jnp.zeros((share, channels), spread.dtype)
    for row in range(3):
        for out_col in range(2):
            for in_col in range(4):
                tap = in_col - out_col
                to = (row * 2 + out_col) * share
                at = in_col * channels
                spread[to : to + share, at : at + channels] = (
                    blocks[row * 3 + tap] if 0 <= tap <= 2 else empty
                )
    sums[...] = jnp.zeros_like(sums)
    if last:
        start_border(cols, side, other_in, other, other_sems)
        lower = half_of_band()
        wait_border(cols, side, other_in, other, other_sems)
        for edge, message in enumerate((east, west, across)):
            first, step = edge_place(own_turn[0], lower, edge, side)
            for pos in range(side):
                pixel = first + pos * step
                place = slice(pos * batch, (pos + 1) * batch)
                sums[pixel + cols] += message[0:share, place].astype(jnp.float32)
                other[pixel] = (
                    other[pixel].astype(jnp.float32)
                    + message[share:, place].astype(jnp.float32)
                ).astype(other.dtype)
        start_border(cols, side, other, other_out, back_sems)

    def add_row(row):
        for start in range(0, cols, 4):
            right = jnp.concatenate(
                [
                    jnp.concatenate(
                        [
                            padded[
                                row,
                                :,
                                (start + half + col) * batch : (start + half + col + 1) * batch,
                            ]
                            for half in (0, 2)
                        ],
                        axis=1,
                    )
                    for col in range(4)
                ],
                axis=0,
            )
            terms = dot(spread[...], right, FLAT)
            for half in (0, 2):
                for col in range(2):
                    part = [
                        terms[
                            (k * 2 + col) * share : (k * 2 + col + 1) * share,
                            half // 2 * batch : (half // 2 + 1) * batch,
                        ]
                        for k in range(3)
                    ]
                    at = start + half + col
                    pixel = row * cols + at
                    sums[pixel + 2 * cols] += part[0]
                    sums[pixel + cols] += part[1]
                    done[jnp.maximum(pixel - cols, at)] = (sums[pixel] + part[2]).astype(
                        done.dtype
                    )

    row_copy(0).wait()
    row_copy(ahead).start()
    add_row(0)

    @pl.loop(1, side, unroll=3)
    def _(row):
        @pl.when(row + ahead < side)
        def _():
            row_copy(row + ahead).start()

        row_copy(row).wait()
        add_row(row)
        row_out(row - 1).start()

    for at in range(cols):
        done[(side - 1) * cols + at] = sums[side * cols + at].astype(done.dtype)
    row_out(side - 1).start()
    for row in range(side):
        row_out(row).wait()
    if last:
        wait_border(cols, side, other, other_out, back_sems)


def convolved(source, weight, turn=None, messages=(), other=None):
    side, channels, width = source.shape
    share = weight.shape[1]
    batch = width // side
    pixels = side * side
    last = other is not None
    vmem = pl.BlockSpec(memory_space=pltpu.VMEM)
    smem = pl.BlockSpec(memory_space=pltpu.SMEM)
    anywhere = pl.BlockSpec(memory_space=pl.ANY)
    shape = jax.ShapeDtypeStruct((pixels, share, batch), jnp.bfloat16)
    scratch = [
        pltpu.VMEM((side, channels, width + 2 * batch), jnp.bfloat16),
        pltpu.VMEM((6 * share, 4 * channels), jnp.bfloat16),
        pltpu.VMEM((pixels + 2 * side, share, batch), jnp.float32),
        pltpu.VMEM((pixels, share, batch), jnp.bfloat16),
        pltpu.SemaphoreType.DMA((side,)),
        pltpu.SemaphoreType.DMA((side,)),
    ]
    if last:
        scratch += [
            pltpu.VMEM((pixels, share, batch), jnp.bfloat16),
            pltpu.SemaphoreType.DMA((3,)),
            pltpu.SemaphoreType.DMA((3,)),
        ]

    def body(*refs):
        conv_kernel(last, *refs)

    call = pl.pallas_call(
        body,
        in_specs=[smem] + [vmem] * 3 + [anywhere, vmem, anywhere] if last else [anywhere, vmem],
        out_specs=[anywhere] * 2 if last else anywhere,
        out_shape=[shape] * 2 if last else shape,
        scratch_shapes=scratch,
        input_output_aliases={6: 1} if last else {},
        compiler_params=pltpu.CompilerParams(vmem_limit_bytes=BIG),
        cost_estimate=pl.CostEstimate(
            flops=2400 * source.size, bytes_accessed=3 * source.size, transcendentals=0
        ),
        name="conv" if last else "grad_conv",
    )
    return call(turn, *messages, source, weight, other) if last else call(source, weight)


def sum_over_tiles(total, count):
    bit = 1
    while bit < count:
        left = count // bit

        def other(flip):
            return lax.ppermute(total, "tile", [(i, i ^ flip) for i in range(count)])

        if left % 4 == 0 and left.bit_length() % 2 == 1:
            near, far, farther = other(bit), other(2 * bit), other(3 * bit)
            total = (total + near) + (far + farther)
            bit *= 4
        else:
            total = total + other(bit)
            bit *= 2
    return total


def per_device(tiles, orientation, weight, grad_out):
    batch, side, _, channels = tiles.shape[1:]
    share = weight.shape[3]
    count = lax.axis_size("tile")
    eastward = [(i, (i + 2) % count) for i in range(count)]
    westward = [(i, (i - 2) % count) for i in range(count)]
    acrossward = [(i, i ^ 1) for i in range(count)]

    def exchanged(sends):
        return [
            lax.ppermute(sends[1], "tile", westward),
            lax.ppermute(sends[0], "tile", eastward),
            lax.ppermute(sends[2], "tile", acrossward),
        ]

    own = weight.transpose(0, 1, 3, 2).reshape(9, share, channels)
    weights = [own] + [
        lax.ppermute(own, "chan", [(i, i ^ flip) for i in range(channels // share)])
        for flip in range(1, channels // share)
    ]
    upstream, upstream_edges, *sends = lay_upstream(orientation, grad_out[0], share)
    messages = exchanged(sends)
    field, edges, inner, rowed = lay_field(orientation, weights, tiles[0], upstream)
    scale = 1.0 / math.sqrt(count * batch * side * side)
    total, *sends = seam_filters(
        scale, orientation, edges, upstream_edges, inner, own, rowed, messages
    )
    messages = exchanged(sends)
    grad = convolved(upstream, rowed)
    conv, grad = convolved(field, own, orientation, messages, grad)
    total = sum_over_tiles(total, count)
    shape = (side, side, share, batch)
    conv_out = conv.reshape(shape).transpose(3, 0, 1, 2)[None]
    grad_input = grad.reshape(shape).transpose(3, 0, 1, 2)[None]
    grad_weight = total.reshape(3, 3, share, channels).transpose(0, 1, 3, 2)
    return conv_out, grad_input, grad_weight


def solution(mesh):
    in_specs = (
        P("tile", None, None, None, None),
        P("tile"),
        P(None, None, None, "chan"),
        P("tile", None, None, None, None),
    )
    out_specs = (
        P("tile", None, None, None, "chan"),
        P("tile", None, None, None, "chan"),
        P(None, None, None, "chan"),
    )
    return jax.shard_map(
        per_device, mesh=mesh, in_specs=in_specs, out_specs=out_specs, check_vma=False
    )
```

```python
import math

import jax
import jax.numpy as jnp
from jax import lax
from jax.experimental import pallas as pl
from jax.experimental.pallas import tpu as pltpu
from jax.sharding import PartitionSpec as P

BIG = 56 << 20
AHEAD = 2
EXTRA = 128
FLAT = (((1,), (0,)), ((), ()))
TURNED = (((1,), (1,)), ((), ()))


def dot(left, right, dims):
    return lax.dot_general(left, right, dims, preferred_element_type=jnp.float32)


def stored(turn, row, col, last):

    def chosen(values):
        return jnp.where(
            turn < 2,
            jnp.where(turn == 0, values[0], values[1]),
            jnp.where(turn == 2, values[2], values[3]),
        )

    return (
        chosen((row, last - col, last - row, col)),
        chosen((col, row, last - col, last - row)),
    )


def edge_place(turn, lower, edge, side):
    last = side - 1
    if edge == 0:
        start, after = (0, last), (1, last)
    elif edge == 1:
        start, after = (0, 0), (1, 0)
    else:
        row = last * (1 - lower)
        start, after = (row, 0), (row, 1)
    row, col = stored(turn, *start, last)
    below, beside = stored(turn, *after, last)
    first = row * side + col
    return first, below * side + beside - first


def edge_tap(turn, lower, edge, along, outward):
    if edge == 0:
        cell = (along, 2 if outward else 0)
    elif edge == 1:
        cell = (along, 0 if outward else 2)
    else:
        cell = (2 - 2 * lower if outward else 2 * lower, along)
    row, col = stored(turn, *cell, 2)
    return row * 3 + col


def one_hot(share, channels):
    chan = lax.axis_index("chan").astype(jnp.int32)
    rows = lax.broadcasted_iota(jnp.int32, (share, channels), 0) + chan * share
    cols = lax.broadcasted_iota(jnp.int32, (share, channels), 1)
    return jnp.where(rows == cols, 1.0, 0.0).astype(jnp.bfloat16)


def half_of_band():
    return lax.axis_index("tile").astype(jnp.int32) % 2


def later(value, width):
    empty = jnp.zeros((value.shape[0], width), value.dtype)
    return jnp.concatenate([empty, value[:, :-width]], axis=1)


def earlier(value, width):
    empty = jnp.zeros((value.shape[0], width), value.dtype)
    return jnp.concatenate([value[:, width:], empty], axis=1)


def terms_of(product, share, batch):
    return (
        later(product[:share], batch)
        + product[share : 2 * share]
        + earlier(product[2 * share : 3 * share], batch)
    ).astype(jnp.bfloat16)


def gather_filters(parts, whole):
    taps, share, _ = parts[0].shape
    chan = lax.axis_index("chan").astype(jnp.int32)
    for flip, part in enumerate(parts):
        start = pl.multiple_of((chan ^ flip) * share, share)
        for tap in range(taps):
            whole[tap, pl.ds(start, share)] = part[tap]


def pair_in(source, stage, sems, pair):
    return pltpu.make_async_copy(
        source.at[:, pl.ds(2 * pair, 2)], stage.at[pair], sems.at[pair]
    )


def turned_out(flat, turned, sems, pair):
    part = pl.ds(2 * pair, 2)
    return pltpu.make_async_copy(flat.at[part], turned.at[part], sems.at[pair])


def lay_pair(stage, held, flat, pair):
    _, batch, rows, side, _ = stage.shape
    for row in range(rows):
        block = jnp.swapaxes(stage[pair, :, row], 0, 1)
        held[pl.ds((2 * pair + row) * side, side)] = block
        for col in range(side):
            flat[2 * pair + row, :, col * batch : (col + 1) * batch] = block[col].T


def upstream_kernel(
    own_turn, upstream, turned, edges, east, west, across,
    stage, even, odd, flat, shuffle, in_sems, turned_sems, edge_sems,
):
    pairs, batch, rows, side, channels = stage.shape
    share = east.shape[0]
    group = 256 // side
    for pair in range(AHEAD):
        pair_in(upstream, stage, in_sems, pair).start()
    to = lax.broadcasted_iota(jnp.int32, (256, 256), 0)
    come = lax.broadcasted_iota(jnp.int32, (256, 256), 1)
    moves = (to // group == come % side) & (to % group == come // side)
    shuffle[...] = jnp.where(moves, 1.0, 0.0).astype(jnp.bfloat16)

    def permute(pair, held):
        @pl.when(pair + AHEAD < pairs)
        def _():
            pair_in(upstream, stage, in_sems, pair + AHEAD).start()

        pair_in(upstream, stage, in_sems, pair).wait()
        for start in range(0, batch, group):
            block = jnp.concatenate(
                [
                    stage[pair, start : start + group, row].reshape(256, channels)
                    for row in range(rows)
                ],
                axis=1,
            )
            moved = dot(shuffle[...], block, FLAT).astype(jnp.bfloat16)
            for row in range(rows):
                held[row * side : (row + 1) * side, start : start + group] = moved[
                    :, row * channels : (row + 1) * channels
                ].reshape(side, group, channels)

    def turn_pair(pair, held):
        for row in range(rows):
            for col in range(side):
                flat[2 * pair + row, :, col * batch : (col + 1) * batch] = held[
                    row * side + col
                ].T
        turned_out(flat, turned, turned_sems, pair).start()

    permute(jnp.int32(0), even)

    @pl.loop(0, pairs // 2 - 1)
    def _(step):
        pair = 2 * step
        permute(pair + 1, odd)
        turn_pair(pair, even)
        permute(pair + 2, even)
        turn_pair(pair + 1, odd)

    permute(jnp.int32(pairs - 1), odd)
    turn_pair(pairs - 2, even)
    turn_pair(pairs - 1, odd)

    chan = lax.axis_index("chan").astype(jnp.int32)
    own = pl.ds(pl.multiple_of(chan * share, share), share)
    lower = half_of_band()
    turn = own_turn[0]
    for edge, out in enumerate((east, west, across)):
        first, step = edge_place(turn, lower, edge, side)
        for pos in range(side):
            pixel = first + pos * step
            row = lax.div(pixel, side)
            col = pl.ds(pl.multiple_of(lax.rem(pixel, side) * batch, batch), batch)
            lanes = pl.ds(pos * batch, batch)
            pltpu.make_async_copy(
                flat.at[row, :, col], edges.at[edge, :, lanes], edge_sems.at[edge]
            ).start()
            out[:, lanes] = flat[row, own, col]
        code = jnp.full((share, EXTRA), turn, jnp.int32)
        out[:, side * batch :] = code.astype(jnp.float32).astype(jnp.bfloat16)
    for pair in range(pairs):
        turned_out(flat, turned, turned_sems, pair).wait()
    for edge in range(3):
        pltpu.make_async_copy(flat.at[0], edges.at[edge], edge_sems.at[edge]).wait()


def lay_upstream(turn, upstream, share):
    batch, side, _, channels = upstream.shape
    vmem = pl.BlockSpec(memory_space=pltpu.VMEM)
    anywhere = pl.BlockSpec(memory_space=pl.ANY)
    pairs = side // 2
    turned = jax.ShapeDtypeStruct((side, channels, side * batch), jnp.bfloat16)
    edges = jax.ShapeDtypeStruct((3, channels, side * batch), jnp.bfloat16)
    message = jax.ShapeDtypeStruct((share, side * batch + EXTRA), jnp.bfloat16)
    return pl.pallas_call(
        upstream_kernel,
        in_specs=[pl.BlockSpec(memory_space=pltpu.SMEM), anywhere],
        out_specs=[anywhere] * 2 + [vmem] * 3,
        out_shape=[turned, edges] + [message] * 3,
        scratch_shapes=[
            pltpu.VMEM((pairs, batch, 2, side, channels), jnp.bfloat16),
            pltpu.VMEM((2 * side, batch, channels), jnp.bfloat16),
            pltpu.VMEM((2 * side, batch, channels), jnp.bfloat16),
            pltpu.VMEM(turned.shape, jnp.bfloat16),
            pltpu.VMEM((256, 256), jnp.bfloat16),
            pltpu.SemaphoreType.DMA((pairs,)),
            pltpu.SemaphoreType.DMA((pairs,)),
            pltpu.SemaphoreType.DMA((3,)),
        ],
        compiler_params=pltpu.CompilerParams(vmem_limit_bytes=BIG),
        cost_estimate=pl.CostEstimate(
            flops=1024 * upstream.size, bytes_accessed=4 * upstream.size, transcendentals=0
        ),
        name="lay_upstream",
    )(turn, upstream)


def field_kernel(
    own_turn, weight, other1, other2, other3, field, turned, laid, edges, inner, rowed,
    stage, held, flat, padded, total, whole, in_sems, out_sems, turned_sem, edge_sems,
):
    pairs, batch, rows, side, channels = stage.shape
    share = padded.shape[1]
    width = side * batch
    chan = lax.axis_index("chan").astype(jnp.int32)
    own = pl.ds(pl.multiple_of(chan * share, share), share)
    turned_in = pltpu.make_async_copy(
        turned.at[:, own], padded.at[pl.ds(1, side), :, pl.ds(batch, width)], turned_sem
    )
    pair_in(field, stage, in_sems, 0).start()
    turned_in.start()
    for pair in range(1, AHEAD):
        pair_in(field, stage, in_sems, pair).start()
    padded[0] = jnp.zeros(padded.shape[1:], padded.dtype)
    padded[side + 1] = jnp.zeros(padded.shape[1:], padded.dtype)
    column = jnp.zeros((side, share, batch), padded.dtype)
    padded[1 : side + 1, :, 0:batch] = column
    padded[1 : side + 1, :, width + batch :] = column
    total[...] = jnp.zeros_like(total)

    def lay(pair):
        pair_in(field, stage, in_sems, pair).wait()
        lay_pair(stage, held, flat, pair)
        turned_out(flat, laid, out_sems, pair).start()

    def add_filters(pair):
        cols = 8
        for start in range(0, side, cols):
            right = jnp.concatenate(
                [
                    held[pl.ds((2 * pair + row) * side + start, cols)].reshape(
                        cols * batch, channels
                    )
                    for row in range(rows)
                ],
                axis=1,
            )
            parts = []
            for tap in range(3):
                at = (start + 2 - tap) * batch
                for half in range(2):
                    part = padded[pl.ds(2 * pair + 2 * half, 2), :, at : at + cols * batch]
                    parts.append(part.reshape(2 * share, cols * batch))
            for half in range(2):
                left = jnp.concatenate(parts[3 * half : 3 * half + 3], axis=0)
                total[6 * share * half : 6 * share * (half + 1)] += dot(left, right, FLAT)

    gather_filters((weight, other1, other2, other3), whole)
    pick = one_hot(share, channels)
    for tap in range(9):
        rowed[tap] = dot(pick, whole[tap], TURNED).astype(jnp.bfloat16)
    lay(0)
    turned_in.wait()

    @pl.loop(1, pairs)
    def _(pair):
        @pl.when(pair + AHEAD - 1 < pairs)
        def _():
            pair_in(field, stage, in_sems, pair + AHEAD - 1).start()

        add_filters(pair - 1)
        lay(pair)

    lower = half_of_band()
    turn = own_turn[0]
    for edge in range(3):
        first, step = edge_place(turn, lower, edge, side)
        for pos in range(side):
            pltpu.make_async_copy(
                held.at[first + pos * step], edges.at[edge, pos], edge_sems.at[edge]
            ).start()
    add_filters(pairs - 1)
    for row_tap in range(3):
        for col_tap in range(3):
            value = jnp.zeros((share, channels), jnp.float32)
            for row in range(rows):
                start = col_tap * (rows + 2) * share + (row + 2 - row_tap) * share
                value += total[start : start + share, row * channels : (row + 1) * channels]
            inner[row_tap * 3 + col_tap] = value
    for pair in range(pairs):
        turned_out(flat, laid, out_sems, pair).wait()
    for edge in range(3):
        pltpu.make_async_copy(
            held.at[pl.ds(0, side)], edges.at[edge], edge_sems.at[edge]
        ).wait()


def lay_field(turn, weights, field, turned):
    share = weights[0].shape[1]
    vmem = pl.BlockSpec(memory_space=pltpu.VMEM)
    batch, side, _, channels = field.shape
    anywhere = pl.BlockSpec(memory_space=pl.ANY)
    pairs = side // 2
    laid = jax.ShapeDtypeStruct((side, channels, side * batch), jnp.bfloat16)
    edges = jax.ShapeDtypeStruct((3, side, batch, channels), jnp.bfloat16)
    inner = jax.ShapeDtypeStruct((9, share, channels), jnp.float32)
    return pl.pallas_call(
        field_kernel,
        in_specs=[pl.BlockSpec(memory_space=pltpu.SMEM)]
        + [vmem] * len(weights)
        + [anywhere] * 2,
        out_specs=[anywhere] * 2 + [vmem] * 2,
        out_shape=[laid, edges, inner, jax.ShapeDtypeStruct(inner.shape, jnp.bfloat16)],
        scratch_shapes=[
            pltpu.VMEM((pairs, batch, 2, side, channels), jnp.bfloat16),
            pltpu.VMEM((side * side, batch, channels), jnp.bfloat16),
            pltpu.VMEM(laid.shape, jnp.bfloat16),
            pltpu.VMEM((side + 2, share, (side + 2) * batch), jnp.bfloat16),
            pltpu.VMEM((12 * share, 2 * channels), jnp.float32),
            pltpu.VMEM((9, channels, channels), jnp.bfloat16),
            pltpu.SemaphoreType.DMA((pairs,)),
            pltpu.SemaphoreType.DMA((pairs,)),
            pltpu.SemaphoreType.DMA,
            pltpu.SemaphoreType.DMA((3,)),
        ],
        compiler_params=pltpu.CompilerParams(vmem_limit_bytes=BIG),
        cost_estimate=pl.CostEstimate(
            flops=1800 * field.size, bytes_accessed=5 * field.size, transcendentals=0
        ),
        name="lay_field",
    )(turn, *weights, field, turned)


def seam_kernel(scale, own_turn, edges_in, upstream_in, inner, weight, rowed, *refs):
    messages, out, terms_out = refs[:3], refs[3], refs[4:7]
    edges, upstream_edges, sems = refs[7:]

    def edge_in(edge):
        return (
            pltpu.make_async_copy(edges_in.at[edge], edges.at[edge], sems.at[0, edge]),
            pltpu.make_async_copy(
                upstream_in.at[edge], upstream_edges.at[edge], sems.at[1, edge]
            ),
        )

    for edge in range(3):
        for copy in edge_in(edge):
            copy.start()
    side, batch, channels = edges.shape[1:]
    share = out.shape[1]
    width = side * batch
    lower = half_of_band()
    out[...] = inner[...]
    for edge, message in enumerate(messages):
        turn = jnp.max(message[0:16, width:].astype(jnp.float32)).astype(jnp.int32)
        taps = [edge_tap(turn, lower, edge, d, False) for d in range(3)]
        turned = message[:, 0:width]
        for copy in edge_in(edge):
            copy.wait()
        left = jnp.concatenate([earlier(turned, batch), turned, later(turned, batch)], axis=0)
        pixels = edges[edge].reshape(width, channels)
        terms = dot(left, pixels, FLAT)
        for d in range(3):
            out[taps[d]] += terms[d * share : (d + 1) * share]
        filters = jnp.concatenate([weight[tap] for tap in taps], axis=0)
        terms_out[edge][0:share] = terms_of(dot(filters, pixels, TURNED), share, batch)
        filters = jnp.concatenate(
            [rowed[edge_tap(own_turn[0], lower, edge, 2 - d, True)] for d in range(3)], axis=0
        )
        terms_out[edge][share:] = terms_of(
            dot(filters, upstream_edges[edge], FLAT), share, batch
        )
    out[...] = out[...] * scale


def seam_filters(scale, turn, edges, upstream_edges, inner, weight, rowed, messages):
    _, side, batch, channels = edges.shape
    share = inner.shape[1]
    vmem = pl.BlockSpec(memory_space=pltpu.VMEM)

    def body(*refs):
        seam_kernel(scale, *refs)

    return pl.pallas_call(
        body,
        in_specs=[pl.BlockSpec(memory_space=pltpu.SMEM)]
        + [pl.BlockSpec(memory_space=pl.ANY)] * 2
        + [vmem] * 6,
        out_specs=[vmem] * 4,
        scratch_shapes=[
            pltpu.VMEM(edges.shape, jnp.bfloat16),
            pltpu.VMEM(upstream_edges.shape, jnp.bfloat16),
            pltpu.SemaphoreType.DMA((2, 3)),
        ],
        out_shape=[jax.ShapeDtypeStruct(inner.shape, jnp.float32)]
        + [jax.ShapeDtypeStruct((2 * share, side * batch), jnp.bfloat16)] * 3,
        compiler_params=pltpu.CompilerParams(vmem_limit_bytes=BIG),
        cost_estimate=pl.CostEstimate(
            flops=54 * share * side * batch * channels,
            bytes_accessed=12 * side * batch * channels,
            transcendentals=0,
        ),
        name="seam_filters",
    )(turn, edges, upstream_edges, inner, weight, rowed, *messages)


def border_rows(cols, rows, source, target, sems):
    copies = []
    for index, row in enumerate((0, rows - 1)):
        where = pl.ds(row * cols, cols)
        copies.append(
            pltpu.make_async_copy(source.at[where], target.at[where], sems.at[index])
        )
    return copies


def start_border(cols, rows, source, target, sems):
    for copy in border_rows(cols, rows, source, target, sems):
        copy.start()
    for row in range(1, rows - 1):
        for col in (0, cols - 1):
            where = pl.ds(row * cols + col, 1)
            pltpu.make_async_copy(source.at[where], target.at[where], sems.at[2]).start()


def wait_border(cols, rows, source, target, sems):
    for copy in border_rows(cols, rows, source, target, sems):
        copy.wait()
    between = pl.ds(cols, 2 * (rows - 2))
    pltpu.make_async_copy(source.at[between], target.at[between], sems.at[2]).wait()


def conv_kernel(last, *refs):
    if last:
        own_turn, east, west, across, source, weight, other_in = refs[:7]
        out, other_out, padded, spread, sums, done, sems, out_sems = refs[7:15]
        other, other_sems, back_sems = refs[15:]
    else:
        source, weight, out, padded, spread, sums, done, sems, out_sems = refs
    side, channels, lanes = padded.shape
    share, batch = done.shape[1:]
    cols = lanes // batch - 2
    ahead = 3

    def row_copy(row):
        return pltpu.make_async_copy(
            source.at[row], padded.at[row, :, pl.ds(batch, cols * batch)], sems.at[row]
        )

    def row_out(row):
        pixels = pl.ds(row * cols, cols)
        return pltpu.make_async_copy(done.at[pixels], out.at[pixels], out_sems.at[row])

    for row in range(ahead):
        row_copy(row).start()
    tile = jnp.zeros((channels, batch), padded.dtype)
    for row in range(side):
        padded[row, :, 0:batch] = tile
        padded[row, :, lanes - batch :] = tile

    blocks = [weight[tap if last else 8 - tap] for tap in range(9)]
    empty = jnp.zeros((share, channels), spread.dtype)
    for row in range(3):
        for out_col in range(2):
            for in_col in range(4):
                tap = in_col - out_col
                to = (row * 2 + out_col) * share
                at = in_col * channels
                spread[to : to + share, at : at + channels] = (
                    blocks[row * 3 + tap] if 0 <= tap <= 2 else empty
                )
    sums[...] = jnp.zeros_like(sums)
    if last:
        start_border(cols, side, other_in, other, other_sems)
        lower = half_of_band()
        edges = [edge_place(own_turn[0], lower, edge, side) for edge in range(3)]
        for (first, step), message in zip(edges, (east, west, across)):
            for pos in range(side):
                place = slice(pos * batch, (pos + 1) * batch)
                sums[first + pos * step + cols] += message[0:share, place].astype(jnp.float32)
        wait_border(cols, side, other_in, other, other_sems)
        for (first, step), message in zip(edges, (east, west, across)):
            for pos in range(side):
                pixel = first + pos * step
                place = slice(pos * batch, (pos + 1) * batch)
                other[pixel] = (
                    other[pixel].astype(jnp.float32)
                    + message[share:, place].astype(jnp.float32)
                ).astype(other.dtype)
        start_border(cols, side, other, other_out, back_sems)

    def add_row(row):
        for start in range(0, cols, 4):
            right = jnp.concatenate(
                [
                    jnp.concatenate(
                        [
                            padded[
                                row,
                                :,
                                (start + half + col) * batch : (start + half + col + 1) * batch,
                            ]
                            for half in (0, 2)
                        ],
                        axis=1,
                    )
                    for col in range(4)
                ],
                axis=0,
            )
            terms = dot(spread[...], right, FLAT)
            for half in (0, 2):
                for col in range(2):
                    part = [
                        terms[
                            (k * 2 + col) * share : (k * 2 + col + 1) * share,
                            half // 2 * batch : (half // 2 + 1) * batch,
                        ]
                        for k in range(3)
                    ]
                    at = start + half + col
                    pixel = row * cols + at
                    sums[pixel + 2 * cols] += part[0]
                    sums[pixel + cols] += part[1]
                    done[jnp.maximum(pixel - cols, at)] = (sums[pixel] + part[2]).astype(
                        done.dtype
                    )

    row_copy(0).wait()
    row_copy(ahead).start()
    add_row(0)

    @pl.loop(1, side, unroll=3)
    def _(row):
        @pl.when(row + ahead < side)
        def _():
            row_copy(row + ahead).start()

        row_copy(row).wait()
        add_row(row)
        row_out(row - 1).start()

    for at in range(cols):
        done[(side - 1) * cols + at] = sums[side * cols + at].astype(done.dtype)
    row_out(side - 1).start()
    for row in range(side):
        row_out(row).wait()
    if last:
        wait_border(cols, side, other, other_out, back_sems)


def convolved(source, weight, turn=None, messages=(), other=None):
    side, channels, width = source.shape
    share = weight.shape[1]
    batch = width // side
    pixels = side * side
    last = other is not None
    vmem = pl.BlockSpec(memory_space=pltpu.VMEM)
    smem = pl.BlockSpec(memory_space=pltpu.SMEM)
    anywhere = pl.BlockSpec(memory_space=pl.ANY)
    shape = jax.ShapeDtypeStruct((pixels, share, batch), jnp.bfloat16)
    scratch = [
        pltpu.VMEM((side, channels, width + 2 * batch), jnp.bfloat16),
        pltpu.VMEM((6 * share, 4 * channels), jnp.bfloat16),
        pltpu.VMEM((pixels + 2 * side, share, batch), jnp.float32),
        pltpu.VMEM((pixels, share, batch), jnp.bfloat16),
        pltpu.SemaphoreType.DMA((side,)),
        pltpu.SemaphoreType.DMA((side,)),
    ]
    if last:
        scratch += [
            pltpu.VMEM((pixels, share, batch), jnp.bfloat16),
            pltpu.SemaphoreType.DMA((3,)),
            pltpu.SemaphoreType.DMA((3,)),
        ]

    def body(*refs):
        conv_kernel(last, *refs)

    call = pl.pallas_call(
        body,
        in_specs=[smem] + [vmem] * 3 + [anywhere, vmem, anywhere] if last else [anywhere, vmem],
        out_specs=[anywhere] * 2 if last else anywhere,
        out_shape=[shape] * 2 if last else shape,
        scratch_shapes=scratch,
        input_output_aliases={6: 1} if last else {},
        compiler_params=pltpu.CompilerParams(vmem_limit_bytes=BIG),
        cost_estimate=pl.CostEstimate(
            flops=2400 * source.size, bytes_accessed=3 * source.size, transcendentals=0
        ),
        name="conv" if last else "grad_conv",
    )
    return call(turn, *messages, source, weight, other) if last else call(source, weight)


def sum_over_tiles(total, count):
    bit = 1
    while bit < count:
        left = count // bit

        def other(flip):
            return lax.ppermute(total, "tile", [(i, i ^ flip) for i in range(count)])

        if left % 4 == 0 and left.bit_length() % 2 == 1:
            near, far, farther = other(bit), other(2 * bit), other(3 * bit)
            total = (total + near) + (far + farther)
            bit *= 4
        else:
            total = total + other(bit)
            bit *= 2
    return total


def per_device(tiles, orientation, weight, grad_out):
    batch, side, _, channels = tiles.shape[1:]
    share = weight.shape[3]
    count = lax.axis_size("tile")
    eastward = [(i, (i + 2) % count) for i in range(count)]
    westward = [(i, (i - 2) % count) for i in range(count)]
    acrossward = [(i, i ^ 1) for i in range(count)]

    def exchanged(sends):
        return [
            lax.ppermute(sends[1], "tile", westward),
            lax.ppermute(sends[0], "tile", eastward),
            lax.ppermute(sends[2], "tile", acrossward),
        ]

    own = weight.transpose(0, 1, 3, 2).reshape(9, share, channels)
    weights = [own] + [
        lax.ppermute(own, "chan", [(i, i ^ flip) for i in range(channels // share)])
        for flip in range(1, channels // share)
    ]
    upstream, upstream_edges, *sends = lay_upstream(orientation, grad_out[0], share)
    messages = exchanged(sends)
    field, edges, inner, rowed = lay_field(orientation, weights, tiles[0], upstream)
    scale = 1.0 / math.sqrt(count * batch * side * side)
    total, *sends = seam_filters(
        scale, orientation, edges, upstream_edges, inner, own, rowed, messages
    )
    messages = exchanged(sends)
    grad = convolved(upstream, rowed)
    conv, grad = convolved(field, own, orientation, messages, grad)
    total = sum_over_tiles(total, count)
    shape = (side, side, share, batch)
    conv_out = conv.reshape(shape).transpose(3, 0, 1, 2)[None]
    grad_input = grad.reshape(shape).transpose(3, 0, 1, 2)[None]
    grad_weight = total.reshape(3, 3, share, channels).transpose(0, 1, 3, 2)
    return conv_out, grad_input, grad_weight


def solution(mesh):
    in_specs = (
        P("tile", None, None, None, None),
        P("tile"),
        P(None, None, None, "chan"),
        P("tile", None, None, None, None),
    )
    out_specs = (
        P("tile", None, None, None, "chan"),
        P("tile", None, None, None, "chan"),
        P(None, None, None, "chan"),
    )
    return jax.shard_map(
        per_device, mesh=mesh, in_specs=in_specs, out_specs=out_specs, check_vma=False
    )
```

```python
import math

import jax
import jax.numpy as jnp
from jax import lax
from jax.experimental import pallas as pl
from jax.experimental.pallas import tpu as pltpu
from jax.sharding import PartitionSpec as P

BIG = 56 << 20
AHEAD = 2
EXTRA = 128
FLAT = (((1,), (0,)), ((), ()))
TURNED = (((1,), (1,)), ((), ()))


def dot(left, right, dims):
    return lax.dot_general(left, right, dims, preferred_element_type=jnp.float32)


def stored(turn, row, col, last):

    def chosen(values):
        return jnp.where(
            turn < 2,
            jnp.where(turn == 0, values[0], values[1]),
            jnp.where(turn == 2, values[2], values[3]),
        )

    return (
        chosen((row, last - col, last - row, col)),
        chosen((col, row, last - col, last - row)),
    )


def edge_place(turn, lower, edge, side):
    last = side - 1
    if edge == 0:
        start, after = (0, last), (1, last)
    elif edge == 1:
        start, after = (0, 0), (1, 0)
    else:
        row = last * (1 - lower)
        start, after = (row, 0), (row, 1)
    row, col = stored(turn, *start, last)
    below, beside = stored(turn, *after, last)
    first = row * side + col
    return first, below * side + beside - first


def edge_tap(turn, lower, edge, along, outward):
    if edge == 0:
        cell = (along, 2 if outward else 0)
    elif edge == 1:
        cell = (along, 0 if outward else 2)
    else:
        cell = (2 - 2 * lower if outward else 2 * lower, along)
    row, col = stored(turn, *cell, 2)
    return row * 3 + col


def one_hot(share, channels):
    chan = lax.axis_index("chan").astype(jnp.int32)
    rows = lax.broadcasted_iota(jnp.int32, (share, channels), 0) + chan * share
    cols = lax.broadcasted_iota(jnp.int32, (share, channels), 1)
    return jnp.where(rows == cols, 1.0, 0.0).astype(jnp.bfloat16)


def half_of_band():
    return lax.axis_index("tile").astype(jnp.int32) % 2


def later(value, width):
    empty = jnp.zeros((value.shape[0], width), value.dtype)
    return jnp.concatenate([empty, value[:, :-width]], axis=1)


def earlier(value, width):
    empty = jnp.zeros((value.shape[0], width), value.dtype)
    return jnp.concatenate([value[:, width:], empty], axis=1)


def terms_of(product, share, batch):
    return (
        later(product[:share], batch)
        + product[share : 2 * share]
        + earlier(product[2 * share : 3 * share], batch)
    ).astype(jnp.bfloat16)


def gather_filters(tap, parts, whole):
    share = parts[0].shape[1]
    chan = lax.axis_index("chan").astype(jnp.int32)
    for flip, part in enumerate(parts):
        start = pl.multiple_of((chan ^ flip) * share, share)
        whole[tap, pl.ds(start, share)] = part[tap]


def pair_in(source, stage, sems, pair):
    return pltpu.make_async_copy(
        source.at[:, pl.ds(2 * pair, 2)], stage.at[pair], sems.at[pair]
    )


def turned_out(flat, turned, sems, pair):
    part = pl.ds(2 * pair, 2)
    return pltpu.make_async_copy(flat.at[part], turned.at[part], sems.at[pair])


def upstream_kernel(
    own_turn, upstream, turned, edges, east, west, across,
    stage, even, odd, flat, shuffle, in_sems, turned_sems, edge_sems,
):
    pairs, batch, rows, side, channels = stage.shape
    share = east.shape[0]
    group = 256 // side
    for pair in range(AHEAD):
        pair_in(upstream, stage, in_sems, pair).start()
    to = lax.broadcasted_iota(jnp.int32, (256, 256), 0)
    come = lax.broadcasted_iota(jnp.int32, (256, 256), 1)
    moves = (to // group == come % side) & (to % group == come // side)
    shuffle[...] = jnp.where(moves, 1.0, 0.0).astype(jnp.bfloat16)

    def permute(pair, held):
        @pl.when(pair + AHEAD < pairs)
        def _():
            pair_in(upstream, stage, in_sems, pair + AHEAD).start()

        pair_in(upstream, stage, in_sems, pair).wait()
        for start in range(0, batch, group):
            block = jnp.concatenate(
                [
                    stage[pair, start : start + group, row].reshape(256, channels)
                    for row in range(rows)
                ],
                axis=1,
            )
            moved = dot(shuffle[...], block, FLAT).astype(jnp.bfloat16)
            for row in range(rows):
                held[row * side : (row + 1) * side, start : start + group] = moved[
                    :, row * channels : (row + 1) * channels
                ].reshape(side, group, channels)

    def turn_pair(pair, held):
        for row in range(rows):
            for col in range(side):
                flat[2 * pair + row, :, col * batch : (col + 1) * batch] = held[
                    row * side + col
                ].T
        turned_out(flat, turned, turned_sems, pair).start()

    permute(jnp.int32(0), even)

    @pl.loop(0, pairs // 2 - 1)
    def _(step):
        pair = 2 * step
        permute(pair + 1, odd)
        turn_pair(pair, even)
        permute(pair + 2, even)
        turn_pair(pair + 1, odd)

    permute(jnp.int32(pairs - 1), odd)
    turn_pair(pairs - 2, even)
    turn_pair(pairs - 1, odd)

    chan = lax.axis_index("chan").astype(jnp.int32)
    own = pl.ds(pl.multiple_of(chan * share, share), share)
    lower = half_of_band()
    turn = own_turn[0]
    for edge, out in enumerate((east, west, across)):
        first, step = edge_place(turn, lower, edge, side)
        for pos in range(side):
            pixel = first + pos * step
            row = lax.div(pixel, side)
            col = pl.ds(pl.multiple_of(lax.rem(pixel, side) * batch, batch), batch)
            lanes = pl.ds(pos * batch, batch)
            pltpu.make_async_copy(
                flat.at[row, :, col], edges.at[edge, :, lanes], edge_sems.at[edge]
            ).start()
            out[:, lanes] = flat[row, own, col]
        code = jnp.full((share, EXTRA), turn, jnp.int32)
        out[:, side * batch :] = code.astype(jnp.float32).astype(jnp.bfloat16)
    for pair in range(pairs):
        turned_out(flat, turned, turned_sems, pair).wait()
    for edge in range(3):
        pltpu.make_async_copy(flat.at[0], edges.at[edge], edge_sems.at[edge]).wait()


def lay_upstream(turn, upstream, share):
    batch, side, _, channels = upstream.shape
    vmem = pl.BlockSpec(memory_space=pltpu.VMEM)
    anywhere = pl.BlockSpec(memory_space=pl.ANY)
    pairs = side // 2
    turned = jax.ShapeDtypeStruct((side, channels, side * batch), jnp.bfloat16)
    edges = jax.ShapeDtypeStruct((3, channels, side * batch), jnp.bfloat16)
    message = jax.ShapeDtypeStruct((share, side * batch + EXTRA), jnp.bfloat16)
    return pl.pallas_call(
        upstream_kernel,
        in_specs=[pl.BlockSpec(memory_space=pltpu.SMEM), anywhere],
        out_specs=[anywhere] * 2 + [vmem] * 3,
        out_shape=[turned, edges] + [message] * 3,
        scratch_shapes=[
            pltpu.VMEM((pairs, batch, 2, side, channels), jnp.bfloat16),
            pltpu.VMEM((2 * side, batch, channels), jnp.bfloat16),
            pltpu.VMEM((2 * side, batch, channels), jnp.bfloat16),
            pltpu.VMEM(turned.shape, jnp.bfloat16),
            pltpu.VMEM((256, 256), jnp.bfloat16),
            pltpu.SemaphoreType.DMA((pairs,)),
            pltpu.SemaphoreType.DMA((pairs,)),
            pltpu.SemaphoreType.DMA((3,)),
        ],
        compiler_params=pltpu.CompilerParams(vmem_limit_bytes=BIG),
        cost_estimate=pl.CostEstimate(
            flops=1024 * upstream.size, bytes_accessed=4 * upstream.size, transcendentals=0
        ),
        name="lay_upstream",
    )(turn, upstream)


def field_kernel(
    own_turn, weight, other1, other2, other3, field, turned, laid, edges, inner, rowed,
    stage, held, even, odd, flat, padded, total, whole,
    in_sems, out_sems, turned_sem, edge_sems,
):
    pairs, batch, rows, side, channels = stage.shape
    share = padded.shape[1]
    width = side * batch
    chan = lax.axis_index("chan").astype(jnp.int32)
    own = pl.ds(pl.multiple_of(chan * share, share), share)
    turned_in = pltpu.make_async_copy(
        turned.at[:, own], padded.at[pl.ds(1, side), :, pl.ds(batch, width)], turned_sem
    )
    pair_in(field, stage, in_sems, 0).start()
    turned_in.start()
    for pair in range(1, AHEAD):
        pair_in(field, stage, in_sems, pair).start()
    padded[0] = jnp.zeros(padded.shape[1:], padded.dtype)
    padded[side + 1] = jnp.zeros(padded.shape[1:], padded.dtype)
    column = jnp.zeros((side, share, batch), padded.dtype)
    padded[1 : side + 1, :, 0:batch] = column
    padded[1 : side + 1, :, width + batch :] = column
    total[...] = jnp.zeros_like(total)

    def lay(pair, block, full_row=None):
        pair_in(field, stage, in_sems, pair).wait()
        for row in range(rows):
            moved = jnp.swapaxes(stage[pair, :, row], 0, 1)
            block[row * side : (row + 1) * side] = moved
            first = (2 * pair + row) * side
            if row == full_row:
                held[pl.ds(first, side)] = moved
            else:
                held[first] = moved[0]
                held[first + side - 1] = moved[side - 1]
            for col in range(side):
                flat[2 * pair + row, :, col * batch : (col + 1) * batch] = moved[col].T
        turned_out(flat, laid, out_sems, pair).start()

    def add_filters(pair, block):
        cols = 8
        for start in range(0, side, cols):
            right = jnp.concatenate(
                [
                    block[row * side + start : row * side + start + cols].reshape(
                        cols * batch, channels
                    )
                    for row in range(rows)
                ],
                axis=1,
            )
            parts = []
            for tap in range(3):
                at = (start + 2 - tap) * batch
                for half in range(2):
                    part = padded[pl.ds(2 * pair + 2 * half, 2), :, at : at + cols * batch]
                    parts.append(part.reshape(2 * share, cols * batch))
            for half in range(2):
                left = jnp.concatenate(parts[3 * half : 3 * half + 3], axis=0)
                total[6 * share * half : 6 * share * (half + 1)] += dot(left, right, FLAT)

    pick = one_hot(share, channels)

    def by_rows(tap):
        gather_filters(tap, (weight, other1, other2, other3), whole)
        rowed[tap] = dot(pick, whole[tap], TURNED).astype(jnp.bfloat16)

    def request(pair):
        @pl.when(pair < pairs)
        def _():
            pair_in(field, stage, in_sems, pair).start()

    lay(0, even, 0)
    turned_in.wait()

    @pl.loop(0, pairs // 2 - 1)
    def _(step):
        pair = 2 * step
        request(pair + AHEAD)
        add_filters(pair, even)
        lay(pair + 1, odd)
        by_rows(pair)
        request(pair + 1 + AHEAD)
        add_filters(pair + 1, odd)
        lay(pair + 2, even)
        by_rows(pair + 1)

    add_filters(pairs - 2, even)
    lay(pairs - 1, odd, rows - 1)
    for tap in range(pairs - 2, 9):
        by_rows(tap)

    lower = half_of_band()
    turn = own_turn[0]
    for edge in range(3):
        first, step = edge_place(turn, lower, edge, side)
        for pos in range(side):
            pltpu.make_async_copy(
                held.at[first + pos * step], edges.at[edge, pos], edge_sems.at[edge]
            ).start()
    add_filters(pairs - 1, odd)
    for row_tap in range(3):
        for col_tap in range(3):
            value = jnp.zeros((share, channels), jnp.float32)
            for row in range(rows):
                start = col_tap * (rows + 2) * share + (row + 2 - row_tap) * share
                value += total[start : start + share, row * channels : (row + 1) * channels]
            inner[row_tap * 3 + col_tap] = value
    for pair in range(pairs):
        turned_out(flat, laid, out_sems, pair).wait()
    for edge in range(3):
        pltpu.make_async_copy(
            held.at[pl.ds(0, side)], edges.at[edge], edge_sems.at[edge]
        ).wait()


def lay_field(turn, weights, field, turned):
    share = weights[0].shape[1]
    vmem = pl.BlockSpec(memory_space=pltpu.VMEM)
    batch, side, _, channels = field.shape
    anywhere = pl.BlockSpec(memory_space=pl.ANY)
    pairs = side // 2
    laid = jax.ShapeDtypeStruct((side, channels, side * batch), jnp.bfloat16)
    edges = jax.ShapeDtypeStruct((3, side, batch, channels), jnp.bfloat16)
    inner = jax.ShapeDtypeStruct((9, share, channels), jnp.float32)
    return pl.pallas_call(
        field_kernel,
        in_specs=[pl.BlockSpec(memory_space=pltpu.SMEM)]
        + [vmem] * len(weights)
        + [anywhere] * 2,
        out_specs=[anywhere] * 2 + [vmem] * 2,
        out_shape=[laid, edges, inner, jax.ShapeDtypeStruct(inner.shape, jnp.bfloat16)],
        scratch_shapes=[
            pltpu.VMEM((pairs, batch, 2, side, channels), jnp.bfloat16),
            pltpu.VMEM((side * side, batch, channels), jnp.bfloat16),
            pltpu.VMEM((2 * side, batch, channels), jnp.bfloat16),
            pltpu.VMEM((2 * side, batch, channels), jnp.bfloat16),
            pltpu.VMEM(laid.shape, jnp.bfloat16),
            pltpu.VMEM((side + 2, share, (side + 2) * batch), jnp.bfloat16),
            pltpu.VMEM((12 * share, 2 * channels), jnp.float32),
            pltpu.VMEM((9, channels, channels), jnp.bfloat16),
            pltpu.SemaphoreType.DMA((pairs,)),
            pltpu.SemaphoreType.DMA((pairs,)),
            pltpu.SemaphoreType.DMA,
            pltpu.SemaphoreType.DMA((3,)),
        ],
        compiler_params=pltpu.CompilerParams(vmem_limit_bytes=BIG),
        cost_estimate=pl.CostEstimate(
            flops=1800 * field.size, bytes_accessed=5 * field.size, transcendentals=0
        ),
        name="lay_field",
    )(turn, *weights, field, turned)


def seam_kernel(scale, own_turn, edges, upstream_edges, inner, weight, rowed, *refs):
    messages, out, terms_out = refs[:3], refs[3], refs[4:7]
    side, batch, channels = edges.shape[1:]
    share = out.shape[1]
    width = side * batch
    lower = half_of_band()
    out[...] = inner[...]
    for edge, message in enumerate(messages):
        turn = jnp.max(message[0:16, width:].astype(jnp.float32)).astype(jnp.int32)
        taps = [edge_tap(turn, lower, edge, d, False) for d in range(3)]
        turned = message[:, 0:width]
        left = jnp.concatenate([earlier(turned, batch), turned, later(turned, batch)], axis=0)
        pixels = edges[edge].reshape(width, channels)
        terms = dot(left, pixels, FLAT)
        for d in range(3):
            out[taps[d]] += terms[d * share : (d + 1) * share]
        filters = jnp.concatenate([weight[tap] for tap in taps], axis=0)
        terms_out[edge][0:share] = terms_of(dot(filters, pixels, TURNED), share, batch)
        filters = jnp.concatenate(
            [rowed[edge_tap(own_turn[0], lower, edge, 2 - d, True)] for d in range(3)], axis=0
        )
        terms_out[edge][share:] = terms_of(
            dot(filters, upstream_edges[edge], FLAT), share, batch
        )
    out[...] = out[...] * scale


def seam_filters(scale, turn, edges, upstream_edges, inner, weight, rowed, messages):
    _, side, batch, channels = edges.shape
    share = inner.shape[1]
    vmem = pl.BlockSpec(memory_space=pltpu.VMEM)

    def body(*refs):
        seam_kernel(scale, *refs)

    return pl.pallas_call(
        body,
        in_specs=[pl.BlockSpec(memory_space=pltpu.SMEM)] + [vmem] * 8,
        out_specs=[vmem] * 4,
        out_shape=[jax.ShapeDtypeStruct(inner.shape, jnp.float32)]
        + [jax.ShapeDtypeStruct((2 * share, side * batch), jnp.bfloat16)] * 3,
        compiler_params=pltpu.CompilerParams(vmem_limit_bytes=BIG),
        cost_estimate=pl.CostEstimate(
            flops=54 * share * side * batch * channels,
            bytes_accessed=12 * side * batch * channels,
            transcendentals=0,
        ),
        name="seam_filters",
    )(turn, edges, upstream_edges, inner, weight, rowed, *messages)


def border_rows(cols, rows, source, target, sems):
    copies = []
    for index, row in enumerate((0, rows - 1)):
        where = pl.ds(row * cols, cols)
        copies.append(
            pltpu.make_async_copy(source.at[where], target.at[where], sems.at[index])
        )
    return copies


def start_border(cols, rows, source, target, sems):
    for copy in border_rows(cols, rows, source, target, sems):
        copy.start()
    for row in range(1, rows - 1):
        for col in (0, cols - 1):
            where = pl.ds(row * cols + col, 1)
            pltpu.make_async_copy(source.at[where], target.at[where], sems.at[2]).start()


def wait_border(cols, rows, source, target, sems):
    for copy in border_rows(cols, rows, source, target, sems):
        copy.wait()
    between = pl.ds(cols, 2 * (rows - 2))
    pltpu.make_async_copy(source.at[between], target.at[between], sems.at[2]).wait()


def conv_kernel(last, *refs):
    if last:
        own_turn, east, west, across, source, weight, other_in = refs[:7]
        out, other_out, padded, spread, sums, done, sems, out_sems = refs[7:15]
        other, other_sems, back_sems = refs[15:]
    else:
        source, weight, out, padded, spread, sums, done, sems, out_sems = refs
    side, channels, lanes = padded.shape
    share, batch = done.shape[1:]
    cols = lanes // batch - 2
    ahead = 3

    def row_copy(row):
        return pltpu.make_async_copy(
            source.at[row], padded.at[row, :, pl.ds(batch, cols * batch)], sems.at[row]
        )

    def row_out(row):
        pixels = pl.ds(row * cols, cols)
        return pltpu.make_async_copy(done.at[pixels], out.at[pixels], out_sems.at[row])

    for row in range(ahead):
        row_copy(row).start()
    tile = jnp.zeros((channels, batch), padded.dtype)
    for row in range(side):
        padded[row, :, 0:batch] = tile
        padded[row, :, lanes - batch :] = tile

    blocks = [weight[tap if last else 8 - tap] for tap in range(9)]
    empty = jnp.zeros((share, channels), spread.dtype)
    for row in range(3):
        for out_col in range(2):
            for in_col in range(4):
                tap = in_col - out_col
                to = (row * 2 + out_col) * share
                at = in_col * channels
                spread[to : to + share, at : at + channels] = (
                    blocks[row * 3 + tap] if 0 <= tap <= 2 else empty
                )
    sums[...] = jnp.zeros_like(sums)
    if last:
        start_border(cols, side, other_in, other, other_sems)
        lower = half_of_band()
        edges = [edge_place(own_turn[0], lower, edge, side) for edge in range(3)]
        for (first, step), message in zip(edges, (east, west, across)):
            for pos in range(side):
                place = slice(pos * batch, (pos + 1) * batch)
                sums[first + pos * step + cols] += message[0:share, place].astype(jnp.float32)
        wait_border(cols, side, other_in, other, other_sems)
        for (first, step), message in zip(edges, (east, west, across)):
            for pos in range(side):
                pixel = first + pos * step
                place = slice(pos * batch, (pos + 1) * batch)
                other[pixel] = (
                    other[pixel].astype(jnp.float32)
                    + message[share:, place].astype(jnp.float32)
                ).astype(other.dtype)
        start_border(cols, side, other, other_out, back_sems)

    def add_row(row):
        for start in range(0, cols, 4):
            right = jnp.concatenate(
                [
                    jnp.concatenate(
                        [
                            padded[
                                row,
                                :,
                                (start + half + col) * batch : (start + half + col + 1) * batch,
                            ]
                            for half in (0, 2)
                        ],
                        axis=1,
                    )
                    for col in range(4)
                ],
                axis=0,
            )
            terms = dot(spread[...], right, FLAT)
            for half in (0, 2):
                for col in range(2):
                    part = [
                        terms[
                            (k * 2 + col) * share : (k * 2 + col + 1) * share,
                            half // 2 * batch : (half // 2 + 1) * batch,
                        ]
                        for k in range(3)
                    ]
                    at = start + half + col
                    pixel = row * cols + at
                    sums[pixel + 2 * cols] += part[0]
                    sums[pixel + cols] += part[1]
                    done[jnp.maximum(pixel - cols, at)] = (sums[pixel] + part[2]).astype(
                        done.dtype
                    )

    row_copy(0).wait()
    row_copy(ahead).start()
    add_row(0)

    @pl.loop(1, side, unroll=3)
    def _(row):
        @pl.when(row + ahead < side)
        def _():
            row_copy(row + ahead).start()

        row_copy(row).wait()
        add_row(row)
        row_out(row - 1).start()

    for at in range(cols):
        done[(side - 1) * cols + at] = sums[side * cols + at].astype(done.dtype)
    row_out(side - 1).start()
    for row in range(side):
        row_out(row).wait()
    if last:
        wait_border(cols, side, other, other_out, back_sems)


def convolved(source, weight, turn=None, messages=(), other=None):
    side, channels, width = source.shape
    share = weight.shape[1]
    batch = width // side
    pixels = side * side
    last = other is not None
    vmem = pl.BlockSpec(memory_space=pltpu.VMEM)
    smem = pl.BlockSpec(memory_space=pltpu.SMEM)
    anywhere = pl.BlockSpec(memory_space=pl.ANY)
    shape = jax.ShapeDtypeStruct((pixels, share, batch), jnp.bfloat16)
    scratch = [
        pltpu.VMEM((side, channels, width + 2 * batch), jnp.bfloat16),
        pltpu.VMEM((6 * share, 4 * channels), jnp.bfloat16),
        pltpu.VMEM((pixels + 2 * side, share, batch), jnp.float32),
        pltpu.VMEM((pixels, share, batch), jnp.bfloat16),
        pltpu.SemaphoreType.DMA((side,)),
        pltpu.SemaphoreType.DMA((side,)),
    ]
    if last:
        scratch += [
            pltpu.VMEM((pixels, share, batch), jnp.bfloat16),
            pltpu.SemaphoreType.DMA((3,)),
            pltpu.SemaphoreType.DMA((3,)),
        ]

    def body(*refs):
        conv_kernel(last, *refs)

    call = pl.pallas_call(
        body,
        in_specs=[smem] + [vmem] * 3 + [anywhere, vmem, anywhere] if last else [anywhere, vmem],
        out_specs=[anywhere] * 2 if last else anywhere,
        out_shape=[shape] * 2 if last else shape,
        scratch_shapes=scratch,
        input_output_aliases={6: 1} if last else {},
        compiler_params=pltpu.CompilerParams(vmem_limit_bytes=BIG),
        cost_estimate=pl.CostEstimate(
            flops=2400 * source.size, bytes_accessed=3 * source.size, transcendentals=0
        ),
        name="conv" if last else "grad_conv",
    )
    return call(turn, *messages, source, weight, other) if last else call(source, weight)


def sum_over_tiles(total, count):
    bit = 1
    while bit < count:
        left = count // bit

        def other(flip):
            return lax.ppermute(total, "tile", [(i, i ^ flip) for i in range(count)])

        if left % 4 == 0 and left.bit_length() % 2 == 1:
            near, far, farther = other(bit), other(2 * bit), other(3 * bit)
            total = (total + near) + (far + farther)
            bit *= 4
        else:
            total = total + other(bit)
            bit *= 2
    return total


def per_device(tiles, orientation, weight, grad_out):
    batch, side, _, channels = tiles.shape[1:]
    share = weight.shape[3]
    count = lax.axis_size("tile")
    eastward = [(i, (i + 2) % count) for i in range(count)]
    westward = [(i, (i - 2) % count) for i in range(count)]
    acrossward = [(i, i ^ 1) for i in range(count)]

    def exchanged(sends):
        return [
            lax.ppermute(sends[1], "tile", westward),
            lax.ppermute(sends[0], "tile", eastward),
            lax.ppermute(sends[2], "tile", acrossward),
        ]

    own = weight.transpose(0, 1, 3, 2).reshape(9, share, channels)
    weights = [own] + [
        lax.ppermute(own, "chan", [(i, i ^ flip) for i in range(channels // share)])
        for flip in range(1, channels // share)
    ]
    upstream, upstream_edges, *sends = lay_upstream(orientation, grad_out[0], share)
    messages = exchanged(sends)
    field, edges, inner, rowed = lay_field(orientation, weights, tiles[0], upstream)
    scale = 1.0 / math.sqrt(count * batch * side * side)
    total, *sends = seam_filters(
        scale, orientation, edges, upstream_edges, inner, own, rowed, messages
    )
    messages = exchanged(sends)
    grad = convolved(upstream, rowed)
    conv, grad = convolved(field, own, orientation, messages, grad)
    total = sum_over_tiles(total, count)
    shape = (side, side, share, batch)
    conv_out = conv.reshape(shape).transpose(3, 0, 1, 2)[None]
    grad_input = grad.reshape(shape).transpose(3, 0, 1, 2)[None]
    grad_weight = total.reshape(3, 3, share, channels).transpose(0, 1, 3, 2)
    return conv_out, grad_input, grad_weight


def solution(mesh):
    in_specs = (
        P("tile", None, None, None, None),
        P("tile"),
        P(None, None, None, "chan"),
        P("tile", None, None, None, None),
    )
    out_specs = (
        P("tile", None, None, None, "chan"),
        P("tile", None, None, None, "chan"),
        P(None, None, None, "chan"),
    )
    return jax.shard_map(
        per_device, mesh=mesh, in_specs=in_specs, out_specs=out_specs, check_vma=False
    )
```
